32 devices in a mesh: seq: 8 (over y, x, core), head: 4 (over z).
Axes of the slice: x: 2, y: 2, z: 4, core: 2. Of those that a mesh axis runs over, the one named last changes fastest.
Arguments:
- queries: bfloat16 [8192, 4096], P('seq', 'head'), may hold values from -6 to 6
- key_states: bfloat16 [8192, 2048], P('seq', 'head'), may hold values from -6 to 6
- value_states: bfloat16 [8192, 2048], P('seq', 'head'), may hold values from -6 to 6
- outputs: bfloat16 [8192, 4096], P('seq', 'head'), may hold values from -6 to 6
- out_grad: bfloat16 [8192, 4096], P(('seq', 'head')), may hold values from -96 to 96
- log_norm: float32 [32, 8192], P('head', 'seq'), may hold values from 6 to 7.6
Outputs:
- query_grad: bfloat16 [8192, 4096], P(('seq', 'head'))
- key_grad: bfloat16 [8192, 2048], P(('seq', 'head'))
- value_grad: bfloat16 [8192, 2048], P(('seq', 'head'))
The draws below stay inside these ranges and needn't reach their ends.
All inputs are finite; a program needn't handle non-finite values.
Results may differ from the reference program's by a relative error of at most 0.0049.
Values may be sent and summed in bfloat16 or wider, within the bound.
A program may use at most 128 MiB of HBM per device.

```python
import jax
import jax.numpy as jnp
from jax import lax

HEADS = 32
KV_HEADS = 16
HEAD_DIM = 128
WINDOW = 1024
LOCAL_TOK = 1024
SLAB = 8192


def block_scale(rng, shape, pieces, least, top_value):
    def one(axis_at, blocks):
        steps = jax.random.uniform(jax.random.fold_in(jax.random.fold_in(rng, 6), axis_at), (blocks,), jnp.float32, least / len(pieces), top_value / len(pieces))
        return jnp.repeat(jnp.exp(steps), shape[axis_at] // blocks).reshape((-1,) + (1,) * (len(shape) - axis_at - 1))

    level = one(*pieces[0])
    for cut in pieces[1:]:
        level = level * one(*cut)
    return level


def gaussian(rng, shape, scale, reach, pieces=(), held_as=jnp.bfloat16):
    drawn = scale * jax.random.normal(rng, shape, jnp.float32)
    if pieces:
        drawn = drawn * block_scale(rng, shape, pieces, -0.22, 0.18)
    return jnp.clip(drawn, -reach, reach).astype(held_as)


def setup_inputs(seed: int = 0) -> dict:
    arg_keys = jax.random.split(jax.random.key(seed), 7)
    queries = gaussian(arg_keys[0], (SLAB, HEADS * HEAD_DIM), 1.0, 6.0, ((0, 8), (1, 4)))
    key_states = gaussian(arg_keys[1], (SLAB, KV_HEADS * HEAD_DIM), 1.0, 6.0, ((0, 8), (1, 4)))
    value_states = gaussian(arg_keys[2], (SLAB, KV_HEADS * HEAD_DIM), 1.0, 6.0, ((0, 8), (1, 4)))
    outputs = gaussian(arg_keys[3], (SLAB, HEADS * HEAD_DIM), 1.0, 6.0, ((0, 8), (1, 4)))
    out_grad = gaussian(arg_keys[4], (SLAB, HEADS * HEAD_DIM), 16.0, 96.0, ((0, 32),))
    log_norm = jnp.clip(6.0 + 1.5999999 * jax.random.uniform(arg_keys[5], (HEADS, SLAB), jnp.float32) ** block_scale(arg_keys[5], (HEADS, SLAB), ((0, 4), (1, 8)), -0.2, 0.2), 6.0, 7.6)
    return dict(queries=queries, key_states=key_states, value_states=value_states, outputs=outputs, out_grad=out_grad, log_norm=log_norm)


score_scale = 168.0 ** -0.5


def reference(queries, key_states, value_states, outputs, out_grad, log_norm):
    seq_total = queries.shape[0]
    group_size = HEADS // KV_HEADS
    block_rows = min(512, LOCAL_TOK)
    block_count = seq_total // block_rows
    query_split = queries.reshape(seq_total, KV_HEADS, group_size, HEAD_DIM)
    grad_split = out_grad.reshape(seq_total, KV_HEADS, group_size, HEAD_DIM)
    grad_delta = jnp.sum(out_grad.astype(jnp.float32).reshape(seq_total, HEADS, HEAD_DIM) * outputs.astype(jnp.float32).reshape(seq_total, HEADS, HEAD_DIM), axis=2).T
    zeros_rim = jnp.zeros((WINDOW, KV_HEADS, HEAD_DIM), key_states.dtype)
    key_padded = jnp.concatenate([zeros_rim, key_states.reshape(seq_total, KV_HEADS, HEAD_DIM)], 0)
    value_padded = jnp.concatenate([zeros_rim, value_states.reshape(seq_total, KV_HEADS, HEAD_DIM)], 0)
    span_rows = WINDOW + block_rows

    def one_block(carried, block_index):
        grad_k_all, grad_v_all = carried
        row_start = block_index * block_rows
        q_rows = lax.dynamic_slice_in_dim(query_split, row_start, block_rows, 0).astype(jnp.float32)
        g_rows = lax.dynamic_slice_in_dim(grad_split, row_start, block_rows, 0).astype(jnp.float32)
        key_rows = lax.dynamic_slice_in_dim(key_padded, row_start, span_rows, 0).astype(jnp.float32)
        value_rows = lax.dynamic_slice_in_dim(value_padded, row_start, span_rows, 0).astype(jnp.float32)
        norm_rows = lax.dynamic_slice_in_dim(log_norm, row_start, block_rows, 1).reshape(KV_HEADS, group_size, block_rows)
        delta_rows = lax.dynamic_slice_in_dim(grad_delta, row_start, block_rows, 1).reshape(KV_HEADS, group_size, block_rows)
        scores = jnp.einsum("qhgd,khd->hgqk", q_rows, key_rows) * score_scale
        query_pos = row_start + jnp.arange(block_rows, dtype=jnp.int32)[:, None]
        key_pos = row_start - WINDOW + jnp.arange(span_rows, dtype=jnp.int32)[None, :]
        offset_gap = query_pos - key_pos
        allowed = (offset_gap >= 0) & (offset_gap < WINDOW) & (key_pos >= 0)
        probability = jnp.where(allowed, jnp.exp(scores - norm_rows[..., None]), 0.0)
        probs_low = lax.optimization_barrier(probability.astype(jnp.bfloat16)).astype(jnp.float32)
        grad_prob = jnp.einsum("qhgd,khd->hgqk", g_rows, value_rows)
        grad_score = lax.optimization_barrier((probability * (grad_prob - delta_rows[..., None])).astype(jnp.bfloat16)).astype(jnp.float32)
        grad_q = jnp.einsum("hgqk,khd->qhgd", grad_score, key_rows) * score_scale
        grad_k = jnp.einsum("hgqk,qhgd->khd", grad_score, q_rows) * score_scale
        grad_v = jnp.einsum("hgqk,qhgd->khd", probs_low, g_rows)
        old_k = lax.dynamic_slice_in_dim(grad_k_all, row_start, span_rows, 0)
        old_v = lax.dynamic_slice_in_dim(grad_v_all, row_start, span_rows, 0)
        grad_k_all = lax.dynamic_update_slice_in_dim(grad_k_all, old_k + grad_k, row_start, 0)
        grad_v_all = lax.dynamic_update_slice_in_dim(grad_v_all, old_v + grad_v, row_start, 0)
        return (grad_k_all, grad_v_all), grad_q.reshape(block_rows, HEADS * HEAD_DIM).astype(jnp.bfloat16)

    initial = (jnp.zeros((WINDOW + seq_total, KV_HEADS, HEAD_DIM), jnp.float32), jnp.zeros((WINDOW + seq_total, KV_HEADS, HEAD_DIM), jnp.float32))
    carried, grad_q_blocks = lax.scan(one_block, initial, jnp.arange(block_count, dtype=jnp.int32))
    grad_k_all, grad_v_all = carried
    query_grad = grad_q_blocks.reshape(seq_total, HEADS * HEAD_DIM)
    key_grad = grad_k_all[WINDOW:].reshape(seq_total, KV_HEADS * HEAD_DIM).astype(jnp.bfloat16)
    value_grad = grad_v_all[WINDOW:].reshape(seq_total, KV_HEADS * HEAD_DIM).astype(jnp.bfloat16)
    return (query_grad, key_grad, value_grad)
```

```python
import functools
import math

import jax
import jax.numpy as jnp
from jax import lax
from jax.experimental import pallas as pl
from jax.experimental.pallas import tpu as pltpu
from jax.sharding import PartitionSpec as P

HEAD_DIM = 128
WINDOW = 1024
BLOCK = 256
AHEAD = 2

score_scale = 168.0 ** (-0.5)
LOG2E = math.log2(math.e)
MESH = pl.DeviceIdType.MESH


def at(start, size, step=None):
    return pl.ds(pl.multiple_of(start, size if step is None else step), size)


def dot(a, b, dims):
    return lax.dot_general(a, b, (dims, ((), ())), preferred_element_type=jnp.float32)


def kernel(
    seqs, heads, groups, ratio, tokens,
    q_hbm, k_hbm, v_hbm, o_hbm, g_hbm, n_hbm,
    dq_hbm, dk_hbm, dv_hbm,
    q_buf, o_buf, g_buf, k_ext, v_ext, norm, stats, k_turned, dq_turned,
    sums, rims, dq_buf, dkv_buf,
    in_sem, norm_sem, g_send, g_recv, kv_send, kv_recv, rim_send, rim_recv,
    dq_send, dq_recv, dkv_send, dkv_recv,
):
    s, z = lax.axis_index("seq"), lax.axis_index("head")
    owned = tokens // heads
    pair = ratio * HEAD_DIM
    q_blocks, rim_blocks = tokens // BLOCK, WINDOW // BLOCK
    has_before, has_after = s > 0, s < seqs - 1

    def inputs(g):
        wide, narrow = at(g * pair, pair), at(g * HEAD_DIM, HEAD_DIM)
        own = pl.ds(WINDOW, tokens)
        return [
            pltpu.make_async_copy(q_hbm.at[:, wide], q_buf.at[g], in_sem.at[g, 0]),
            pltpu.make_async_copy(o_hbm.at[:, wide], o_buf.at[g], in_sem.at[g, 1]),
            pltpu.make_async_copy(k_hbm.at[:, narrow], k_ext.at[g, own], in_sem.at[g, 2]),
            pltpu.make_async_copy(v_hbm.at[:, narrow], v_ext.at[g, own], in_sem.at[g, 3]),
            pltpu.make_async_copy(
                g_hbm.at[:, at(z * groups * pair + g * pair, pair)],
                g_buf.at[g, at(z * owned, owned)],
                in_sem.at[g, 4],
            ),
        ]

    def grad_in(g, d):
        peer = lax.rem(z + d, heads)
        return pltpu.make_async_remote_copy(
            src_ref=g_hbm.at[:, at(peer * groups * pair + g * pair, pair)],
            dst_ref=g_buf.at[g, at(z * owned, owned)],
            send_sem=g_send.at[g, d],
            recv_sem=g_recv.at[g, d],
            device_id={"head": peer},
            device_id_type=MESH,
        )

    def window_in(g, c):
        src, dst = ((k_hbm, k_ext), (v_hbm, v_ext))[c]
        return pltpu.make_async_remote_copy(
            src_ref=src.at[pl.ds(tokens - WINDOW, WINDOW), at(g * HEAD_DIM, HEAD_DIM)],
            dst_ref=dst.at[g, pl.ds(0, WINDOW)],
            send_sem=kv_send.at[g, c],
            recv_sem=kv_recv.at[g, c],
            device_id={"seq": s + 1},
            device_id_type=MESH,
        )

    def rim_out(g):
        return pltpu.make_async_remote_copy(
            src_ref=sums.at[g, :, pl.ds(0, WINDOW)],
            dst_ref=rims.at[g],
            send_sem=rim_send.at[g],
            recv_sem=rim_recv.at[g],
            device_id={"seq": s - 1},
            device_id_type=MESH,
        )

    def dq_out(g, d):
        peer = lax.rem(z + d, heads)
        return pltpu.make_async_remote_copy(
            src_ref=dq_buf.at[g, at(peer * owned, owned)],
            dst_ref=dq_hbm.at[:, at(z * groups * pair + g * pair, pair)],
            send_sem=dq_send.at[g, d],
            recv_sem=dq_recv.at[g, d],
            device_id={"head": peer},
            device_id_type=MESH,
        )

    def dq_own(g):
        return pltpu.make_async_copy(
            dq_buf.at[g, at(z * owned, owned)],
            dq_hbm.at[:, at(z * groups * pair + g * pair, pair)],
            dq_send.at[g, 0],
        )

    def dkv_out(g, c, d):
        peer = lax.rem(z + d, heads)
        return pltpu.make_async_remote_copy(
            src_ref=dkv_buf.at[g, c, at(peer * owned, owned)],
            dst_ref=(dk_hbm, dv_hbm)[c].at[:, at((z * groups + g) * HEAD_DIM, HEAD_DIM)],
            send_sem=dkv_send.at[g, c, d],
            recv_sem=dkv_recv.at[g, c, d],
            device_id={"head": peer},
            device_id_type=MESH,
        )

    def dkv_own(g, c):
        return pltpu.make_async_copy(
            dkv_buf.at[g, c, at(z * owned, owned)],
            (dk_hbm, dv_hbm)[c].at[:, at((z * groups + g) * HEAD_DIM, HEAD_DIM)],
            dkv_send.at[g, c, 0],
        )

    def send_grads(g):
        for d in range(1, heads):
            grad_in(g, d).start()

    def send_windows(g):
        @pl.when(has_after)
        def _():
            for c in range(2):
                window_in(g, c).start()

    def tile(g, j, i, in_rim):
        keys, rows = at(j * BLOCK, BLOCK), at(i * BLOCK, BLOCK)
        k_rows, v_rows, k_cols = k_ext[g, keys, :], v_ext[g, keys, :], k_turned[:, keys]
        ahead = lax.broadcasted_iota(jnp.int32, (BLOCK, BLOCK), 1) - lax.broadcasted_iota(
            jnp.int32, (BLOCK, BLOCK), 0
        )
        allowed = None
        if in_rim or q_blocks > rim_blocks:
            allowed = ahead < jnp.where(i < j, BLOCK, 0)
        if not in_rim:
            later = ahead >= jnp.where(i > j - rim_blocks, -BLOCK, 0)
            allowed = later if allowed is None else allowed & later
        dk = dv = None
        for h in range(ratio):
            lanes = slice(h * HEAD_DIM, (h + 1) * HEAD_DIM)
            q_rows, g_rows = q_buf[g, rows, lanes], g_buf[g, rows, lanes]
            scores = dot(k_rows, q_rows, ((1,), (1,)))
            probs = jnp.exp2(scores * (score_scale * LOG2E) - stats[h : h + 1, rows])
            probs = jnp.where(allowed, probs, 0.0)
            grad_prob = dot(v_rows, g_rows, ((1,), (1,)))
            grad_score = (
                probs * (grad_prob - stats[ratio + h : ratio + h + 1, rows])
            ).astype(jnp.bfloat16)
            dv_h = dot(probs.astype(jnp.bfloat16), g_rows, ((1,), (0,)))
            dk_h = dot(grad_score, q_rows, ((1,), (0,)))
            dq_turned[h, :, rows] += dot(k_cols, grad_score, ((1,), (0,)))
            dk = dk_h if dk is None else dk + dk_h
            dv = dv_h if dv is None else dv + dv_h
        sums[g, 0, keys, :] += dk
        sums[g, 1, keys, :] += dv

    def key_block(g, j, in_rim):
        keys = at(j * BLOCK, BLOCK)
        k_turned[:, keys] = k_ext[g, keys, :].astype(jnp.float32).T.astype(jnp.bfloat16)
        sums[g, :, keys, :] = jnp.zeros((2, BLOCK, HEAD_DIM), jnp.float32)
        low, high = jnp.maximum(j - rim_blocks, 0), jnp.minimum(j + 1, q_blocks)
        lax.fori_loop(low, high, lambda i, _: (tile(g, j, i, in_rim), 0)[1], 0)

    def prepare(g):
        ones = jnp.ones((8, HEAD_DIM), jnp.bfloat16)
        for h in range(ratio):
            lanes = slice(h * HEAD_DIM, (h + 1) * HEAD_DIM)
            stats[h : h + 1, :] = norm[pl.ds(g * ratio + h, 1), :] * LOG2E

            def rows_of(i, _, h=h, lanes=lanes):
                rows = at(i * BLOCK, BLOCK)
                both = g_buf[g, rows, lanes].astype(jnp.float32) * o_buf[g, rows, lanes].astype(
                    jnp.float32
                )
                high = both.astype(jnp.bfloat16)
                low = (both - high.astype(jnp.float32)).astype(jnp.bfloat16)
                delta = dot(ones, high, ((1,), (1,))) + dot(ones, low, ((1,), (1,)))
                stats[ratio + h : ratio + h + 1, rows] = delta[0:1, :]
                return 0

            lax.fori_loop(0, q_blocks, rows_of, 0)
            dq_turned[h] = jnp.zeros((HEAD_DIM, tokens), jnp.float32)

    def finish_dq(g):
        def rows_of(i, _):
            rows = at(i * BLOCK, BLOCK)
            for h in range(ratio):
                lanes = slice(h * HEAD_DIM, (h + 1) * HEAD_DIM)
                dq_buf[g, rows, lanes] = (dq_turned[h, :, rows].T * score_scale).astype(
                    jnp.bfloat16
                )
            return 0

        lax.fori_loop(0, q_blocks, rows_of, 0)
        for d in range(1, heads):
            dq_out(g, d).start()
        dq_own(g).start()

    def finish_dkv(g):
        @pl.when(has_after)
        def _():
            rim_out(g).wait_recv()

            def add(i, _):
                rows = at(i * BLOCK, BLOCK)
                own = at(tokens + i * BLOCK, BLOCK)
                for c in range(2):
                    sums[g, c, own, :] += rims[g, c, rows, :]
                return 0

            lax.fori_loop(0, rim_blocks, add, 0)

        def rows_of(i, _):
            rows, own = at(i * BLOCK, BLOCK), at(WINDOW + i * BLOCK, BLOCK)
            dkv_buf[g, 0, rows, :] = (sums[g, 0, own, :] * score_scale).astype(jnp.bfloat16)
            dkv_buf[g, 1, rows, :] = sums[g, 1, own, :].astype(jnp.bfloat16)
            return 0

        lax.fori_loop(0, q_blocks, rows_of, 0)
        for c in range(2):
            for d in range(1, heads):
                dkv_out(g, c, d).start()
            dkv_own(g, c).start()

    norm_in = pltpu.make_async_copy(n_hbm, norm, norm_sem)
    norm_in.start()

    def start_inputs(g, _):
        for copy in inputs(g):
            copy.start()
        return 0

    lax.fori_loop(0, groups, start_inputs, 0)

    barrier = pltpu.get_barrier_semaphore()
    for d in range(1, heads):
        pl.semaphore_signal(
            barrier, inc=1, device_id={"head": lax.rem(z + d, heads)}, device_id_type=MESH
        )

    @pl.when(has_before)
    def _():
        pl.semaphore_signal(barrier, inc=1, device_id={"seq": s - 1}, device_id_type=MESH)

    @pl.when(has_after)
    def _():
        pl.semaphore_signal(barrier, inc=1, device_id={"seq": s + 1}, device_id_type=MESH)

    pl.semaphore_wait(
        barrier, heads - 1 + has_before.astype(jnp.int32) + has_after.astype(jnp.int32)
    )

    for g in range(min(AHEAD, groups)):
        send_grads(g)
        send_windows(g)
    norm_in.wait()

    def one_group(g, _):
        for copy in inputs(g):
            copy.wait()
        for d in range(1, heads):
            grad_in(g, d).wait_recv()

        @pl.when(g + AHEAD < groups)
        def _():
            send_grads(g + AHEAD)
            send_windows(g + AHEAD)

        prepare(g)

        @pl.when(has_before)
        def _():
            for c in range(2):
                window_in(g, c).wait_recv()
            lax.fori_loop(0, rim_blocks, lambda j, _: (key_block(g, j, True), 0)[1], 0)
            rim_out(g).start()

        lax.fori_loop(
            rim_blocks, rim_blocks + q_blocks, lambda j, _: (key_block(g, j, False), 0)[1], 0
        )
        finish_dq(g)

        @pl.when(g > 0)
        def _():
            finish_dkv(g - 1)

        return 0

    lax.fori_loop(0, groups, one_group, 0)
    finish_dkv(groups - 1)

    def drain(g, _):
        for d in range(1, heads):
            grad_in(g, d).wait_send()
            dq_out(g, d).wait()
            for c in range(2):
                dkv_out(g, c, d).wait()
        dq_own(g).wait()
        for c in range(2):
            dkv_own(g, c).wait()

        @pl.when(has_after)
        def _():
            for c in range(2):
                window_in(g, c).wait_send()

        @pl.when(has_before)
        def _():
            rim_out(g).wait_send()

        return 0

    lax.fori_loop(0, groups, drain, 0)


def on_device(seqs, heads, queries, key_states, value_states, outputs, out_grad, log_norm):
    tokens = queries.shape[0]
    groups = key_states.shape[1] // HEAD_DIM
    ratio = queries.shape[1] // key_states.shape[1]
    pair, owned, span = ratio * HEAD_DIM, tokens // heads, WINDOW + tokens
    low, wide = jnp.bfloat16, jnp.float32
    dma = pltpu.SemaphoreType.DMA
    pairs = groups * ratio * tokens * (WINDOW + BLOCK)
    return pl.pallas_call(
        functools.partial(kernel, seqs, heads, groups, ratio, tokens),
        out_shape=(
            jax.ShapeDtypeStruct((owned, out_grad.shape[1]), low),
            jax.ShapeDtypeStruct((owned, key_states.shape[1] * heads), low),
            jax.ShapeDtypeStruct((owned, key_states.shape[1] * heads), low),
        ),
        in_specs=[pl.BlockSpec(memory_space=pl.ANY)] * 6,
        out_specs=[pl.BlockSpec(memory_space=pl.ANY)] * 3,
        scratch_shapes=[
            pltpu.VMEM((groups, tokens, pair), low),
            pltpu.VMEM((groups, tokens, pair), low),
            pltpu.VMEM((groups, tokens, pair), low),
            pltpu.VMEM((groups, span, HEAD_DIM), low),
            pltpu.VMEM((groups, span, HEAD_DIM), low),
            pltpu.VMEM(log_norm.shape, wide),
            pltpu.VMEM((2 * ratio, tokens), wide),
            pltpu.VMEM((HEAD_DIM, span), low),
            pltpu.VMEM((ratio, HEAD_DIM, tokens), wide),
            pltpu.VMEM((groups, 2, span, HEAD_DIM), wide),
            pltpu.VMEM((groups, 2, WINDOW, HEAD_DIM), wide),
            pltpu.VMEM((groups, tokens, pair), low),
            pltpu.VMEM((groups, 2, tokens, HEAD_DIM), low),
            dma((groups, 5)),
            dma,
            dma((groups, heads)),
            dma((groups, heads)),
            dma((groups, 2)),
            dma((groups, 2)),
            dma((groups,)),
            dma((groups,)),
            dma((groups, heads)),
            dma((groups, heads)),
            dma((groups, 2, heads)),
            dma((groups, 2, heads)),
        ],
        cost_estimate=pl.CostEstimate(
            flops=10 * pairs * HEAD_DIM, bytes_accessed=12 * tokens * 1024, transcendentals=pairs
        ),
        compiler_params=pltpu.CompilerParams(
            collective_id=0, has_side_effects=True, vmem_limit_bytes=56 * 1024 * 1024
        ),
    )(queries, key_states, value_states, outputs, out_grad, log_norm)


def solution(mesh):
    placed = (
        P("seq", "head"),
        P("seq", "head"),
        P("seq", "head"),
        P("seq", "head"),
        P(("seq", "head"), None),
        P("head", "seq"),
    )
    return jax.shard_map(
        functools.partial(on_device, mesh.shape["seq"], mesh.shape["head"]),
        mesh=mesh,
        in_specs=placed,
        out_specs=(P(("seq", "head"), None), P(("seq", "head"), None), P(("seq", "head"), None)),
        check_vma=False,
    )
```

```python
import functools
import math

import jax
import jax.numpy as jnp
from jax import lax
from jax.experimental import pallas as pl
from jax.experimental.pallas import tpu as pltpu
from jax.sharding import PartitionSpec as P

HEAD_DIM = 128
WINDOW = 1024
BLOCK = 256
AHEAD = 2

score_scale = 168.0 ** (-0.5)
LOG2E = math.log2(math.e)
MESH = pl.DeviceIdType.MESH


def at(start, size, step=None):
    return pl.ds(pl.multiple_of(start, size if step is None else step), size)


def dot(a, b, dims):
    return lax.dot_general(a, b, (dims, ((), ())), preferred_element_type=jnp.float32)


def kernel(
    seqs, heads, groups, ratio, tokens,
    q_hbm, k_hbm, v_hbm, o_hbm, g_hbm, n_hbm,
    dq_hbm, dk_hbm, dv_hbm,
    q_buf, o_buf, g_buf, k_ext, v_ext, norm, stats, k_turned, dq_turned,
    sums, rims, dq_buf, dkv_buf,
    in_sem, norm_sem, g_send, g_recv, kv_send, kv_recv, rim_send, rim_recv,
    dq_send, dq_recv, dkv_send, dkv_recv,
):
    s, z = lax.axis_index("seq"), lax.axis_index("head")
    owned = tokens // heads
    pair = ratio * HEAD_DIM
    q_blocks, rim_blocks = tokens // BLOCK, WINDOW // BLOCK
    has_before, has_after = s > 0, s < seqs - 1

    in_low = (2 * z < heads).astype(jnp.int32)

    def peer_of(n):
        down, up = heads - 1 - n, jnp.int32(n)
        down -= (down <= z).astype(jnp.int32)
        up += (up >= z).astype(jnp.int32)
        return in_low * down + (1 - in_low) * up

    peers = [peer_of(n) for n in range(heads - 1)]
    mine = heads - 1

    def inputs(g):
        wide, narrow = at(g * pair, pair), at(g * HEAD_DIM, HEAD_DIM)
        own = pl.ds(WINDOW, tokens)
        return [
            pltpu.make_async_copy(q_hbm.at[:, wide], q_buf.at[g], in_sem.at[g, 0]),
            pltpu.make_async_copy(o_hbm.at[:, wide], o_buf.at[g], in_sem.at[g, 1]),
            pltpu.make_async_copy(k_hbm.at[:, narrow], k_ext.at[g, own], in_sem.at[g, 2]),
            pltpu.make_async_copy(v_hbm.at[:, narrow], v_ext.at[g, own], in_sem.at[g, 3]),
            pltpu.make_async_copy(
                g_hbm.at[:, at(z * groups * pair + g * pair, pair)],
                g_buf.at[g, at(z * owned, owned)],
                in_sem.at[g, 4],
            ),
        ]

    def grad_in(g, n, source=None):
        peer = peers[n]
        return pltpu.make_async_remote_copy(
            src_ref=g_hbm.at[:, at(peer * groups * pair + g * pair, pair)],
            dst_ref=g_buf.at[g, at(z * owned, owned)],
            send_sem=g_send.at[g, n],
            recv_sem=g_recv.at[g, z if source is None else source],
            device_id={"head": peer},
            device_id_type=MESH,
        )

    def window_in(g, c):
        src, dst = ((k_hbm, k_ext), (v_hbm, v_ext))[c]
        return pltpu.make_async_remote_copy(
            src_ref=src.at[pl.ds(tokens - WINDOW, WINDOW), at(g * HEAD_DIM, HEAD_DIM)],
            dst_ref=dst.at[g, pl.ds(0, WINDOW)],
            send_sem=kv_send.at[g, c],
            recv_sem=kv_recv.at[g, c],
            device_id={"seq": s + 1},
            device_id_type=MESH,
        )

    def rim_out(g):
        return pltpu.make_async_remote_copy(
            src_ref=sums.at[g, :, pl.ds(0, WINDOW)],
            dst_ref=rims.at[g],
            send_sem=rim_send.at[g],
            recv_sem=rim_recv.at[g],
            device_id={"seq": s - 1},
            device_id_type=MESH,
        )

    def dq_out(g, n, source=None):
        peer = peers[n]
        return pltpu.make_async_remote_copy(
            src_ref=dq_buf.at[g, at(peer * owned, owned)],
            dst_ref=dq_hbm.at[:, at(z * groups * pair + g * pair, pair)],
            send_sem=dq_send.at[g, n],
            recv_sem=dq_recv.at[g, z if source is None else source],
            device_id={"head": peer},
            device_id_type=MESH,
        )

    def dq_own(g):
        return pltpu.make_async_copy(
            dq_buf.at[g, at(z * owned, owned)],
            dq_hbm.at[:, at(z * groups * pair + g * pair, pair)],
            dq_send.at[g, mine],
        )

    def dkv_out(g, c, n, source=None):
        peer = peers[n]
        return pltpu.make_async_remote_copy(
            src_ref=dkv_buf.at[g, c, at(peer * owned, owned)],
            dst_ref=(dk_hbm, dv_hbm)[c].at[:, at((z * groups + g) * HEAD_DIM, HEAD_DIM)],
            send_sem=dkv_send.at[g, c, n],
            recv_sem=dkv_recv.at[g, c, z if source is None else source],
            device_id={"head": peer},
            device_id_type=MESH,
        )

    def dkv_own(g, c):
        return pltpu.make_async_copy(
            dkv_buf.at[g, c, at(z * owned, owned)],
            (dk_hbm, dv_hbm)[c].at[:, at((z * groups + g) * HEAD_DIM, HEAD_DIM)],
            dkv_send.at[g, c, mine],
        )

    def send_grads(g):
        for n in range(heads - 1):
            grad_in(g, n).start()

    def send_windows(g):
        @pl.when(has_after)
        def _():
            for c in range(2):
                window_in(g, c).start()

    def tile(g, j, i, in_rim):
        keys, rows = at(j * BLOCK, BLOCK), at(i * BLOCK, BLOCK)
        k_rows, v_rows, k_cols = k_ext[g, keys, :], v_ext[g, keys, :], k_turned[:, keys]
        ahead = lax.broadcasted_iota(jnp.int32, (BLOCK, BLOCK), 1) - lax.broadcasted_iota(
            jnp.int32, (BLOCK, BLOCK), 0
        )
        allowed = None
        if in_rim or q_blocks > rim_blocks:
            allowed = ahead < jnp.where(i < j, BLOCK, 0)
        if not in_rim:
            later = ahead >= jnp.where(i > j - rim_blocks, -BLOCK, 0)
            allowed = later if allowed is None else allowed & later
        dk = dv = None
        for h in range(ratio):
            lanes = slice(h * HEAD_DIM, (h + 1) * HEAD_DIM)
            q_rows, g_rows = q_buf[g, rows, lanes], g_buf[g, rows, lanes]
            scores = dot(k_rows, q_rows, ((1,), (1,)))
            probs = jnp.exp2(scores * (score_scale * LOG2E) - stats[h : h + 1, rows])
            probs = jnp.where(allowed, probs, 0.0)
            grad_prob = dot(v_rows, g_rows, ((1,), (1,)))
            grad_score = (
                probs * (grad_prob - stats[ratio + h : ratio + h + 1, rows])
            ).astype(jnp.bfloat16)
            dv_h = dot(probs.astype(jnp.bfloat16), g_rows, ((1,), (0,)))
            dk_h = dot(grad_score, q_rows, ((1,), (0,)))
            dq_turned[h, :, rows] += dot(k_cols, grad_score, ((1,), (0,)))
            dk = dk_h if dk is None else dk + dk_h
            dv = dv_h if dv is None else dv + dv_h
        sums[g, 0, keys, :] += dk
        sums[g, 1, keys, :] += dv

    def key_block(g, j, in_rim):
        keys = at(j * BLOCK, BLOCK)
        k_turned[:, keys] = k_ext[g, keys, :].astype(jnp.float32).T.astype(jnp.bfloat16)
        sums[g, :, keys, :] = jnp.zeros((2, BLOCK, HEAD_DIM), jnp.float32)
        low, high = jnp.maximum(j - rim_blocks, 0), jnp.minimum(j + 1, q_blocks)
        lax.fori_loop(low, high, lambda i, _: (tile(g, j, i, in_rim), 0)[1], 0)

    def prepare(g):
        ones = jnp.ones((8, HEAD_DIM), jnp.bfloat16)
        for h in range(ratio):
            lanes = slice(h * HEAD_DIM, (h + 1) * HEAD_DIM)
            stats[h : h + 1, :] = norm[pl.ds(g * ratio + h, 1), :] * LOG2E

            def rows_of(i, _, h=h, lanes=lanes):
                rows = at(i * BLOCK, BLOCK)
                both = g_buf[g, rows, lanes].astype(jnp.float32) * o_buf[g, rows, lanes].astype(
                    jnp.float32
                )
                high = both.astype(jnp.bfloat16)
                low = (both - high.astype(jnp.float32)).astype(jnp.bfloat16)
                delta = dot(ones, high, ((1,), (1,))) + dot(ones, low, ((1,), (1,)))
                stats[ratio + h : ratio + h + 1, rows] = delta[0:1, :]
                return 0

            lax.fori_loop(0, q_blocks, rows_of, 0)
            dq_turned[h] = jnp.zeros((HEAD_DIM, tokens), jnp.float32)

    def finish_dq(g):
        def rows_of(i, _):
            rows = at(i * BLOCK, BLOCK)
            for h in range(ratio):
                lanes = slice(h * HEAD_DIM, (h + 1) * HEAD_DIM)
                dq_buf[g, rows, lanes] = (dq_turned[h, :, rows].T * score_scale).astype(
                    jnp.bfloat16
                )
            return 0

        lax.fori_loop(0, q_blocks, rows_of, 0)
        for n in range(heads - 1):
            dq_out(g, n).start()
        dq_own(g).start()

    def finish_dkv(g):
        @pl.when(has_after)
        def _():
            rim_out(g).wait_recv()

            def add(i, _):
                rows = at(i * BLOCK, BLOCK)
                own = at(tokens + i * BLOCK, BLOCK)
                for c in range(2):
                    sums[g, c, own, :] += rims[g, c, rows, :]
                return 0

            lax.fori_loop(0, rim_blocks, add, 0)

        def rows_of(i, _):
            rows, own = at(i * BLOCK, BLOCK), at(WINDOW + i * BLOCK, BLOCK)
            dkv_buf[g, 0, rows, :] = (sums[g, 0, own, :] * score_scale).astype(jnp.bfloat16)
            dkv_buf[g, 1, rows, :] = sums[g, 1, own, :].astype(jnp.bfloat16)
            return 0

        lax.fori_loop(0, q_blocks, rows_of, 0)
        for n in range(heads - 1):
            for c in range(2):
                dkv_out(g, c, n).start()
        for c in range(2):
            dkv_own(g, c).start()

    norm_in = pltpu.make_async_copy(n_hbm, norm, norm_sem)
    norm_in.start()

    def start_inputs(g, _):
        for copy in inputs(g):
            copy.start()
        return 0

    lax.fori_loop(0, groups, start_inputs, 0)

    barrier = pltpu.get_barrier_semaphore()
    for d in range(1, heads):
        pl.semaphore_signal(
            barrier, inc=1, device_id={"head": lax.rem(z + d, heads)}, device_id_type=MESH
        )

    @pl.when(has_before)
    def _():
        pl.semaphore_signal(barrier, inc=1, device_id={"seq": s - 1}, device_id_type=MESH)

    @pl.when(has_after)
    def _():
        pl.semaphore_signal(barrier, inc=1, device_id={"seq": s + 1}, device_id_type=MESH)

    pl.semaphore_wait(
        barrier, heads - 1 + has_before.astype(jnp.int32) + has_after.astype(jnp.int32)
    )

    for g in range(min(AHEAD, groups)):
        send_grads(g)
        send_windows(g)
    norm_in.wait()

    def one_group(g, _):
        for copy in inputs(g):
            copy.wait()
        for n in range(heads - 1):
            grad_in(g, n, peers[n]).wait_recv()

        @pl.when(g + AHEAD < groups)
        def _():
            send_grads(g + AHEAD)
            send_windows(g + AHEAD)

        prepare(g)

        @pl.when(has_before)
        def _():
            for c in range(2):
                window_in(g, c).wait_recv()
            lax.fori_loop(0, rim_blocks, lambda j, _: (key_block(g, j, True), 0)[1], 0)
            rim_out(g).start()

        @pl.when(g > 0)
        def _():
            finish_dkv(g - 1)

        lax.fori_loop(
            rim_blocks, rim_blocks + q_blocks, lambda j, _: (key_block(g, j, False), 0)[1], 0
        )
        finish_dq(g)
        return 0

    lax.fori_loop(0, groups, one_group, 0)
    finish_dkv(groups - 1)

    def drain(g, _):
        for n in range(heads - 1):
            grad_in(g, n).wait_send()
            dq_out(g, n, peers[n]).wait()
            for c in range(2):
                dkv_out(g, c, n, peers[n]).wait()
        dq_own(g).wait()
        for c in range(2):
            dkv_own(g, c).wait()

        @pl.when(has_after)
        def _():
            for c in range(2):
                window_in(g, c).wait_send()

        @pl.when(has_before)
        def _():
            rim_out(g).wait_send()

        return 0

    lax.fori_loop(0, groups, drain, 0)


def write_out(dq, dk, dv, dq_hbm, dk_hbm, dv_hbm, sem):
    copies = [
        pltpu.make_async_copy(src, dst, sem.at[n])
        for n, (src, dst) in enumerate(((dq, dq_hbm), (dk, dk_hbm), (dv, dv_hbm)))
    ]
    for copy in copies:
        copy.start()
    for copy in copies:
        copy.wait()


def on_device(seqs, heads, queries, key_states, value_states, outputs, out_grad, log_norm):
    tokens = queries.shape[0]
    groups = key_states.shape[1] // HEAD_DIM
    ratio = queries.shape[1] // key_states.shape[1]
    pair, owned, span = ratio * HEAD_DIM, tokens // heads, WINDOW + tokens
    low, wide = jnp.bfloat16, jnp.float32
    dma = pltpu.SemaphoreType.DMA
    pairs = groups * ratio * tokens * (WINDOW + BLOCK)
    shapes = [
        (owned, out_grad.shape[1]),
        (owned, key_states.shape[1] * heads),
        (owned, key_states.shape[1] * heads),
    ]
    landed = pl.pallas_call(
        functools.partial(kernel, seqs, heads, groups, ratio, tokens),
        out_shape=[pltpu.VMEM(shape, low) for shape in shapes],
        in_specs=[pl.BlockSpec(memory_space=pltpu.HBM)] * 6,
        out_specs=[pl.BlockSpec(memory_space=pltpu.VMEM)] * 3,
        scratch_shapes=[
            pltpu.VMEM((groups, tokens, pair), low),
            pltpu.VMEM((groups, tokens, pair), low),
            pltpu.VMEM((groups, tokens, pair), low),
            pltpu.VMEM((groups, span, HEAD_DIM), low),
            pltpu.VMEM((groups, span, HEAD_DIM), low),
            pltpu.VMEM(log_norm.shape, wide),
            pltpu.VMEM((2 * ratio, tokens), wide),
            pltpu.VMEM((HEAD_DIM, span), low),
            pltpu.VMEM((ratio, HEAD_DIM, tokens), wide),
            pltpu.VMEM((groups, 2, span, HEAD_DIM), wide),
            pltpu.VMEM((groups, 2, WINDOW, HEAD_DIM), wide),
            pltpu.VMEM((groups, tokens, pair), low),
            pltpu.VMEM((groups, 2, tokens, HEAD_DIM), low),
            dma((groups, 5)),
            dma,
            dma((groups, heads)),
            dma((groups, heads)),
            dma((groups, 2)),
            dma((groups, 2)),
            dma((groups,)),
            dma((groups,)),
            dma((groups, heads)),
            dma((groups, heads)),
            dma((groups, 2, heads)),
            dma((groups, 2, heads)),
        ],
        cost_estimate=pl.CostEstimate(
            flops=10 * pairs * HEAD_DIM, bytes_accessed=12 * tokens * 1024, transcendentals=pairs
        ),
        compiler_params=pltpu.CompilerParams(
            collective_id=0, has_side_effects=True, vmem_limit_bytes=52 * 1024 * 1024
        ),
    )(queries, key_states, value_states, outputs, out_grad, log_norm)
    return pl.pallas_call(
        write_out,
        out_shape=[jax.ShapeDtypeStruct(shape, low) for shape in shapes],
        in_specs=[pl.BlockSpec(memory_space=pltpu.VMEM)] * 3,
        out_specs=[pl.BlockSpec(memory_space=pltpu.HBM)] * 3,
        scratch_shapes=[dma((3,))],
    )(*landed)


def solution(mesh):
    placed = (
        P("seq", "head"),
        P("seq", "head"),
        P("seq", "head"),
        P("seq", "head"),
        P(("seq", "head"), None),
        P("head", "seq"),
    )
    return jax.shard_map(
        functools.partial(on_device, mesh.shape["seq"], mesh.shape["head"]),
        mesh=mesh,
        in_specs=placed,
        out_specs=(P(("seq", "head"), None), P(("seq", "head"), None), P(("seq", "head"), None)),
        check_vma=False,
    )
```

```python
import functools
import math

import jax
import jax.numpy as jnp
from jax import lax
from jax.experimental import pallas as pl
from jax.experimental.pallas import tpu as pltpu
from jax.sharding import PartitionSpec as P

HEAD_DIM = 128
WINDOW = 1024
BLOCK = 256
AHEAD = 3

score_scale = 168.0 ** (-0.5)
LOG2E = math.log2(math.e)
MESH = pl.DeviceIdType.MESH


def at(start, size, step=None):
    return pl.ds(pl.multiple_of(start, size if step is None else step), size)


def dot(a, b, dims):
    return lax.dot_general(a, b, (dims, ((), ())), preferred_element_type=jnp.float32)


def kernel(
    seqs, heads, groups, ratio, tokens,
    q_hbm, k_hbm, v_hbm, o_hbm, g_hbm, n_hbm,
    dq_hbm, dk_hbm, dv_hbm,
    q_buf, o_buf, g_buf, k_ext, v_ext, norm, stats, k_turned, dq_turned,
    sums, rims, dq_buf, dkv_buf,
    in_sem, norm_sem, g_send, g_recv, kv_send, kv_recv, rim_send, rim_recv,
    dq_send, dq_recv, dkv_send, dkv_recv,
):
    s, z = lax.axis_index("seq"), lax.axis_index("head")
    owned = tokens // heads
    pair = ratio * HEAD_DIM
    q_blocks, rim_blocks = tokens // BLOCK, WINDOW // BLOCK
    has_before, has_after = s > 0, s < seqs - 1

    in_low = (2 * z < heads).astype(jnp.int32)

    def peer_of(n):
        down, up = heads - 1 - n, jnp.int32(n)
        down -= (down <= z).astype(jnp.int32)
        up += (up >= z).astype(jnp.int32)
        return in_low * down + (1 - in_low) * up

    peers = [peer_of(n) for n in range(heads - 1)]
    mine = heads - 1

    def inputs(g):
        wide, narrow = at(g * pair, pair), at(g * HEAD_DIM, HEAD_DIM)
        own = pl.ds(WINDOW, tokens)
        return [
            pltpu.make_async_copy(q_hbm.at[:, wide], q_buf.at[g], in_sem.at[g, 0]),
            pltpu.make_async_copy(o_hbm.at[:, wide], o_buf.at[g], in_sem.at[g, 1]),
            pltpu.make_async_copy(k_hbm.at[:, narrow], k_ext.at[g, own], in_sem.at[g, 2]),
            pltpu.make_async_copy(v_hbm.at[:, narrow], v_ext.at[g, own], in_sem.at[g, 3]),
            pltpu.make_async_copy(
                g_hbm.at[:, at(z * groups * pair + g * pair, pair)],
                g_buf.at[g, at(z * owned, owned)],
                in_sem.at[g, 4],
            ),
        ]

    def grad_in(g, n, source=None):
        peer = peers[n]
        return pltpu.make_async_remote_copy(
            src_ref=g_hbm.at[:, at(peer * groups * pair + g * pair, pair)],
            dst_ref=g_buf.at[g, at(z * owned, owned)],
            send_sem=g_send.at[g, n],
            recv_sem=g_recv.at[g, z if source is None else source],
            device_id={"head": peer},
            device_id_type=MESH,
        )

    def window_in(g, c):
        src, dst = ((k_hbm, k_ext), (v_hbm, v_ext))[c]
        return pltpu.make_async_remote_copy(
            src_ref=src.at[pl.ds(tokens - WINDOW, WINDOW), at(g * HEAD_DIM, HEAD_DIM)],
            dst_ref=dst.at[g, pl.ds(0, WINDOW)],
            send_sem=kv_send.at[g, c],
            recv_sem=kv_recv.at[g, c],
            device_id={"seq": s + 1},
            device_id_type=MESH,
        )

    def rim_out(g):
        return pltpu.make_async_remote_copy(
            src_ref=sums.at[g, :, pl.ds(0, WINDOW)],
            dst_ref=rims.at[g],
            send_sem=rim_send.at[g],
            recv_sem=rim_recv.at[g],
            device_id={"seq": s - 1},
            device_id_type=MESH,
        )

    def dq_out(g, n, source=None):
        peer = peers[n]
        return pltpu.make_async_remote_copy(
            src_ref=dq_buf.at[g, at(peer * owned, owned)],
            dst_ref=dq_hbm.at[:, at(z * groups * pair + g * pair, pair)],
            send_sem=dq_send.at[g, n],
            recv_sem=dq_recv.at[g, z if source is None else source],
            device_id={"head": peer},
            device_id_type=MESH,
        )

    def dq_own(g):
        return pltpu.make_async_copy(
            dq_buf.at[g, at(z * owned, owned)],
            dq_hbm.at[:, at(z * groups * pair + g * pair, pair)],
            dq_send.at[g, mine],
        )

    def dkv_out(g, c, n, source=None):
        peer = peers[n]
        return pltpu.make_async_remote_copy(
            src_ref=dkv_buf.at[g, c, at(peer * owned, owned)],
            dst_ref=(dk_hbm, dv_hbm)[c].at[:, at((z * groups + g) * HEAD_DIM, HEAD_DIM)],
            send_sem=dkv_send.at[g, c, n],
            recv_sem=dkv_recv.at[g, c, z if source is None else source],
            device_id={"head": peer},
            device_id_type=MESH,
        )

    def dkv_own(g, c):
        return pltpu.make_async_copy(
            dkv_buf.at[g, c, at(z * owned, owned)],
            (dk_hbm, dv_hbm)[c].at[:, at((z * groups + g) * HEAD_DIM, HEAD_DIM)],
            dkv_send.at[g, c, mine],
        )

    def send_grads(g):
        for n in range(heads - 1):
            grad_in(g, n).start()

    def send_windows(g):
        @pl.when(has_after)
        def _():
            for c in range(2):
                window_in(g, c).start()

    def tile(g, j, i, in_rim):
        keys, rows = at(j * BLOCK, BLOCK), at(i * BLOCK, BLOCK)
        k_rows, v_rows, k_cols = k_ext[g, keys, :], v_ext[g, keys, :], k_turned[:, keys]
        ahead = lax.broadcasted_iota(jnp.int32, (BLOCK, BLOCK), 1) - lax.broadcasted_iota(
            jnp.int32, (BLOCK, BLOCK), 0
        )
        allowed = None
        if in_rim or q_blocks > rim_blocks:
            allowed = ahead < jnp.where(i < j, BLOCK, 0)
        if not in_rim:
            later = ahead >= jnp.where(i > j - rim_blocks, -BLOCK, 0)
            allowed = later if allowed is None else allowed & later
        dk = dv = None
        for h in range(ratio):
            lanes = slice(h * HEAD_DIM, (h + 1) * HEAD_DIM)
            q_rows, g_rows = q_buf[g, rows, lanes], g_buf[g, rows, lanes]
            scores = dot(k_rows, q_rows, ((1,), (1,)))
            probs = jnp.exp2(scores * (score_scale * LOG2E) - stats[h : h + 1, rows])
            probs = jnp.where(allowed, probs, 0.0)
            grad_prob = dot(v_rows, g_rows, ((1,), (1,)))
            grad_score = (
                probs * (grad_prob - stats[ratio + h : ratio + h + 1, rows])
            ).astype(jnp.bfloat16)
            dv_h = dot(probs.astype(jnp.bfloat16), g_rows, ((1,), (0,)))
            dk_h = dot(grad_score, q_rows, ((1,), (0,)))
            dq_turned[h, :, rows] += dot(k_cols, grad_score, ((1,), (0,)))
            dk = dk_h if dk is None else dk + dk_h
            dv = dv_h if dv is None else dv + dv_h
        sums[g, 0, keys, :] += dk
        sums[g, 1, keys, :] += dv

    def key_block(g, j, in_rim):
        keys = at(j * BLOCK, BLOCK)
        k_turned[:, keys] = k_ext[g, keys, :].astype(jnp.float32).T.astype(jnp.bfloat16)
        sums[g, :, keys, :] = jnp.zeros((2, BLOCK, HEAD_DIM), jnp.float32)
        low, high = jnp.maximum(j - rim_blocks, 0), jnp.minimum(j + 1, q_blocks)
        lax.fori_loop(low, high, lambda i, _: (tile(g, j, i, in_rim), 0)[1], 0)

    def prepare(g):
        ones = jnp.ones((8, HEAD_DIM), jnp.bfloat16)
        for h in range(ratio):
            lanes = slice(h * HEAD_DIM, (h + 1) * HEAD_DIM)
            stats[h : h + 1, :] = norm[pl.ds(g * ratio + h, 1), :] * LOG2E

            def rows_of(i, _, h=h, lanes=lanes):
                rows = at(i * BLOCK, BLOCK)
                both = g_buf[g, rows, lanes].astype(jnp.float32) * o_buf[g, rows, lanes].astype(
                    jnp.float32
                )
                high = both.astype(jnp.bfloat16)
                low = (both - high.astype(jnp.float32)).astype(jnp.bfloat16)
                delta = dot(ones, high, ((1,), (1,))) + dot(ones, low, ((1,), (1,)))
                stats[ratio + h : ratio + h + 1, rows] = delta[0:1, :]
                return 0

            lax.fori_loop(0, q_blocks, rows_of, 0)
            dq_turned[h] = jnp.zeros((HEAD_DIM, tokens), jnp.float32)

    def finish_dq(g):
        def rows_of(i, _):
            rows = at(i * BLOCK, BLOCK)
            for h in range(ratio):
                lanes = slice(h * HEAD_DIM, (h + 1) * HEAD_DIM)
                dq_buf[g, rows, lanes] = (dq_turned[h, :, rows].T * score_scale).astype(
                    jnp.bfloat16
                )
            return 0

        lax.fori_loop(0, q_blocks, rows_of, 0)
        for n in range(heads - 1):
            dq_out(g, n).start()
        dq_own(g).start()

    def finish_dkv(g):
        @pl.when(has_after)
        def _():
            rim_out(g).wait_recv()

            def add(i, _):
                rows = at(i * BLOCK, BLOCK)
                own = at(tokens + i * BLOCK, BLOCK)
                for c in range(2):
                    sums[g, c, own, :] += rims[g, c, rows, :]
                return 0

            lax.fori_loop(0, rim_blocks, add, 0)

        def rows_of(i, _):
            rows, own = at(i * BLOCK, BLOCK), at(WINDOW + i * BLOCK, BLOCK)
            dkv_buf[g, 0, rows, :] = (sums[g, 0, own, :] * score_scale).astype(jnp.bfloat16)
            dkv_buf[g, 1, rows, :] = sums[g, 1, own, :].astype(jnp.bfloat16)
            return 0

        lax.fori_loop(0, q_blocks, rows_of, 0)
        for n in range(heads - 1):
            for c in range(2):
                dkv_out(g, c, n).start()
        for c in range(2):
            dkv_own(g, c).start()

    norm_in = pltpu.make_async_copy(n_hbm, norm, norm_sem)
    norm_in.start()

    def start_inputs(g, _):
        for copy in inputs(g):
            copy.start()
        return 0

    lax.fori_loop(0, groups, start_inputs, 0)

    barrier = pltpu.get_barrier_semaphore()
    for d in range(1, heads):
        pl.semaphore_signal(
            barrier, inc=1, device_id={"head": lax.rem(z + d, heads)}, device_id_type=MESH
        )

    @pl.when(has_before)
    def _():
        pl.semaphore_signal(barrier, inc=1, device_id={"seq": s - 1}, device_id_type=MESH)

    @pl.when(has_after)
    def _():
        pl.semaphore_signal(barrier, inc=1, device_id={"seq": s + 1}, device_id_type=MESH)

    pl.semaphore_wait(
        barrier, heads - 1 + has_before.astype(jnp.int32) + has_after.astype(jnp.int32)
    )

    for g in range(min(AHEAD, groups)):
        send_grads(g)
        send_windows(g)
    norm_in.wait()

    def one_group(g, _):
        for copy in inputs(g):
            copy.wait()
        for n in range(heads - 1):
            grad_in(g, n, peers[n]).wait_recv()

        @pl.when(g + AHEAD < groups)
        def _():
            send_grads(g + AHEAD)
            send_windows(g + AHEAD)

        prepare(g)

        @pl.when(has_before)
        def _():
            for c in range(2):
                window_in(g, c).wait_recv()
            lax.fori_loop(0, rim_blocks, lambda j, _: (key_block(g, j, True), 0)[1], 0)
            rim_out(g).start()

        @pl.when(g > 0)
        def _():
            finish_dkv(g - 1)

        lax.fori_loop(
            rim_blocks, rim_blocks + q_blocks, lambda j, _: (key_block(g, j, False), 0)[1], 0
        )
        finish_dq(g)
        return 0

    lax.fori_loop(0, groups, one_group, 0)
    finish_dkv(groups - 1)

    def drain(g, _):
        for n in range(heads - 1):
            grad_in(g, n).wait_send()
            dq_out(g, n, peers[n]).wait()
            for c in range(2):
                dkv_out(g, c, n, peers[n]).wait()
        dq_own(g).wait()
        for c in range(2):
            dkv_own(g, c).wait()

        @pl.when(has_after)
        def _():
            for c in range(2):
                window_in(g, c).wait_send()

        @pl.when(has_before)
        def _():
            rim_out(g).wait_send()

        return 0

    lax.fori_loop(0, groups, drain, 0)


def write_out(dq, dk, dv, dq_hbm, dk_hbm, dv_hbm, sem):
    copies = []
    for src, dst, parts in ((dq, dq_hbm, 4), (dk, dk_hbm, 2), (dv, dv_hbm, 2)):
        size = src.shape[0] // parts
        for n in range(parts):
            rows = pl.ds(n * size, size)
            copies.append(pltpu.make_async_copy(src.at[rows], dst.at[rows], sem.at[len(copies)]))
    for copy in copies:
        copy.start()
    for copy in copies:
        copy.wait()


def on_device(seqs, heads, queries, key_states, value_states, outputs, out_grad, log_norm):
    tokens = queries.shape[0]
    groups = key_states.shape[1] // HEAD_DIM
    ratio = queries.shape[1] // key_states.shape[1]
    pair, owned, span = ratio * HEAD_DIM, tokens // heads, WINDOW + tokens
    low, wide = jnp.bfloat16, jnp.float32
    dma = pltpu.SemaphoreType.DMA
    pairs = groups * ratio * tokens * (WINDOW + BLOCK)
    shapes = [
        (owned, out_grad.shape[1]),
        (owned, key_states.shape[1] * heads),
        (owned, key_states.shape[1] * heads),
    ]
    landed = pl.pallas_call(
        functools.partial(kernel, seqs, heads, groups, ratio, tokens),
        out_shape=[pltpu.VMEM(shape, low) for shape in shapes],
        in_specs=[pl.BlockSpec(memory_space=pltpu.HBM)] * 6,
        out_specs=[pl.BlockSpec(memory_space=pltpu.VMEM)] * 3,
        scratch_shapes=[
            pltpu.VMEM((groups, tokens, pair), low),
            pltpu.VMEM((groups, tokens, pair), low),
            pltpu.VMEM((groups, tokens, pair), low),
            pltpu.VMEM((groups, span, HEAD_DIM), low),
            pltpu.VMEM((groups, span, HEAD_DIM), low),
            pltpu.VMEM(log_norm.shape, wide),
            pltpu.VMEM((2 * ratio, tokens), wide),
            pltpu.VMEM((HEAD_DIM, span), low),
            pltpu.VMEM((ratio, HEAD_DIM, tokens), wide),
            pltpu.VMEM((groups, 2, span, HEAD_DIM), wide),
            pltpu.VMEM((groups, 2, WINDOW, HEAD_DIM), wide),
            pltpu.VMEM((groups, tokens, pair), low),
            pltpu.VMEM((groups, 2, tokens, HEAD_DIM), low),
            dma((groups, 5)),
            dma,
            dma((groups, heads)),
            dma((groups, heads)),
            dma((groups, 2)),
            dma((groups, 2)),
            dma((groups,)),
            dma((groups,)),
            dma((groups, heads)),
            dma((groups, heads)),
            dma((groups, 2, heads)),
            dma((groups, 2, heads)),
        ],
        cost_estimate=pl.CostEstimate(
            flops=10 * pairs * HEAD_DIM, bytes_accessed=12 * tokens * 1024, transcendentals=pairs
        ),
        compiler_params=pltpu.CompilerParams(
            collective_id=0, has_side_effects=True, vmem_limit_bytes=52 * 1024 * 1024
        ),
    )(queries, key_states, value_states, outputs, out_grad, log_norm)
    return pl.pallas_call(
        write_out,
        out_shape=[jax.ShapeDtypeStruct(shape, low) for shape in shapes],
        in_specs=[pl.BlockSpec(memory_space=pl.ANY)] * 3,
        out_specs=[pl.BlockSpec(memory_space=pltpu.HBM)] * 3,
        scratch_shapes=[dma((8,))],
        compiler_params=pltpu.CompilerParams(vmem_limit_bytes=1024 * 1024),
    )(*landed)


def solution(mesh):
    placed = (
        P("seq", "head"),
        P("seq", "head"),
        P("seq", "head"),
        P("seq", "head"),
        P(("seq", "head"), None),
        P("head", "seq"),
    )
    return jax.shard_map(
        functools.partial(on_device, mesh.shape["seq"], mesh.shape["head"]),
        mesh=mesh,
        in_specs=placed,
        out_specs=(P(("seq", "head"), None), P(("seq", "head"), None), P(("seq", "head"), None)),
        check_vma=False,
    )
```

```python
import functools
import math

import jax
import jax.numpy as jnp
from jax import lax
from jax.experimental import pallas as pl
from jax.experimental.pallas import tpu as pltpu
from jax.sharding import PartitionSpec as P

HEAD_DIM = 128
WINDOW = 1024
BLOCK = 256
AHEAD = 3

score_scale = 168.0 ** (-0.5)
LOG2E = math.log2(math.e)
MESH = pl.DeviceIdType.MESH


def at(start, size, step=None):
    return pl.ds(pl.multiple_of(start, size if step is None else step), size)


def dot(a, b, dims):
    return lax.dot_general(a, b, (dims, ((), ())), preferred_element_type=jnp.float32)


def kernel(
    seqs, heads, groups, ratio, tokens,
    q_hbm, k_hbm, v_hbm, o_hbm, g_hbm, n_hbm,
    dq_land, dkv_land,
    q_buf, o_buf, g_buf, k_ext, v_ext, norm, stats, k_turned, dq_turned,
    sums, rims, dq_buf, dkv_buf, staged,
    in_sem, norm_sem, stage_sem, g_send, g_recv, kv_send, kv_recv, rim_send, rim_recv,
    dq_send, dq_recv, dkv_send, dkv_recv,
):
    s, z = lax.axis_index("seq"), lax.axis_index("head")
    owned = tokens // heads
    pair = ratio * HEAD_DIM
    q_blocks, rim_blocks = tokens // BLOCK, WINDOW // BLOCK
    has_before, has_after = s > 0, s < seqs - 1

    in_low = (2 * z < heads).astype(jnp.int32)

    def peer_of(n):
        down, up = heads - 1 - n, jnp.int32(n)
        down -= (down <= z).astype(jnp.int32)
        up += (up >= z).astype(jnp.int32)
        return in_low * down + (1 - in_low) * up

    peers = [peer_of(n) for n in range(heads - 1)]
    mine = heads - 1

    def inputs(g):
        wide, narrow = at(g * pair, pair), at(g * HEAD_DIM, HEAD_DIM)
        own = pl.ds(WINDOW, tokens)
        return [
            pltpu.make_async_copy(q_hbm.at[:, wide], q_buf.at[g], in_sem.at[g, 0]),
            pltpu.make_async_copy(o_hbm.at[:, wide], o_buf.at[g], in_sem.at[g, 1]),
            pltpu.make_async_copy(k_hbm.at[:, narrow], k_ext.at[g, own], in_sem.at[g, 2]),
            pltpu.make_async_copy(v_hbm.at[:, narrow], v_ext.at[g, own], in_sem.at[g, 3]),
            pltpu.make_async_copy(
                g_hbm.at[:, at(z * groups * pair + g * pair, pair)],
                g_buf.at[g, at(z * owned, owned)],
                in_sem.at[g, 4],
            ),
        ]

    def stage(g, n):
        return pltpu.make_async_copy(
            g_hbm.at[:, at(peers[n] * groups * pair + g * pair, pair)],
            staged.at[g, n],
            stage_sem.at[g, n],
        )

    def grad_in(g, n, source=None):
        return pltpu.make_async_remote_copy(
            src_ref=staged.at[g, n],
            dst_ref=g_buf.at[g, at(z * owned, owned)],
            send_sem=g_send.at[g, n],
            recv_sem=g_recv.at[g, z if source is None else source],
            device_id={"head": peers[n]},
            device_id_type=MESH,
        )

    def window_in(g, c):
        src, dst = ((k_hbm, k_ext), (v_hbm, v_ext))[c]
        return pltpu.make_async_remote_copy(
            src_ref=src.at[pl.ds(tokens - WINDOW, WINDOW), at(g * HEAD_DIM, HEAD_DIM)],
            dst_ref=dst.at[g, pl.ds(0, WINDOW)],
            send_sem=kv_send.at[g, c],
            recv_sem=kv_recv.at[g, c],
            device_id={"seq": s + 1},
            device_id_type=MESH,
        )

    def rim_out(g):
        return pltpu.make_async_remote_copy(
            src_ref=sums.at[g, :, pl.ds(0, WINDOW)],
            dst_ref=rims.at[g],
            send_sem=rim_send.at[g],
            recv_sem=rim_recv.at[g],
            device_id={"seq": s - 1},
            device_id_type=MESH,
        )

    def dq_out(g, n, source=None):
        return pltpu.make_async_remote_copy(
            src_ref=dq_buf.at[g, at(peers[n] * owned, owned)],
            dst_ref=dq_land.at[z * groups + g],
            send_sem=dq_send.at[g, n],
            recv_sem=dq_recv.at[g, z if source is None else source],
            device_id={"head": peers[n]},
            device_id_type=MESH,
        )

    def dq_own(g):
        return pltpu.make_async_copy(
            dq_buf.at[g, at(z * owned, owned)], dq_land.at[z * groups + g], dq_send.at[g, mine]
        )

    def dkv_out(g, n, source=None):
        return pltpu.make_async_remote_copy(
            src_ref=dkv_buf.at[g, peers[n]],
            dst_ref=dkv_land.at[z * groups + g],
            send_sem=dkv_send.at[g, n],
            recv_sem=dkv_recv.at[g, z if source is None else source],
            device_id={"head": peers[n]},
            device_id_type=MESH,
        )

    def dkv_own(g):
        return pltpu.make_async_copy(
            dkv_buf.at[g, z], dkv_land.at[z * groups + g], dkv_send.at[g, mine]
        )

    def send_grads(g):
        for n in range(heads - 1):
            stage(g, n).wait()
            grad_in(g, n).start()

    def send_windows(g):
        @pl.when(has_after)
        def _():
            for c in range(2):
                window_in(g, c).start()

    def tile(g, j, i, in_rim):
        keys, rows = at(j * BLOCK, BLOCK), at(i * BLOCK, BLOCK)
        k_rows, v_rows, k_cols = k_ext[g, keys, :], v_ext[g, keys, :], k_turned[:, keys]
        ahead = lax.broadcasted_iota(jnp.int32, (BLOCK, BLOCK), 1) - lax.broadcasted_iota(
            jnp.int32, (BLOCK, BLOCK), 0
        )
        allowed = None
        if in_rim or q_blocks > rim_blocks:
            allowed = ahead < jnp.where(i < j, BLOCK, 0)
        if not in_rim:
            later = ahead >= jnp.where(i > j - rim_blocks, -BLOCK, 0)
            allowed = later if allowed is None else allowed & later
        dk = dv = None
        for h in range(ratio):
            lanes = slice(h * HEAD_DIM, (h + 1) * HEAD_DIM)
            q_rows, g_rows = q_buf[g, rows, lanes], g_buf[g, rows, lanes]
            scores = dot(k_rows, q_rows, ((1,), (1,)))
            probs = jnp.exp2(scores * (score_scale * LOG2E) - stats[h : h + 1, rows])
            probs = jnp.where(allowed, probs, 0.0)
            grad_prob = dot(v_rows, g_rows, ((1,), (1,)))
            grad_score = (
                probs * (grad_prob - stats[ratio + h : ratio + h + 1, rows])
            ).astype(jnp.bfloat16)
            dv_h = dot(probs.astype(jnp.bfloat16), g_rows, ((1,), (0,)))
            dk_h = dot(grad_score, q_rows, ((1,), (0,)))
            dq_turned[h, :, rows] += dot(k_cols, grad_score, ((1,), (0,)))
            dk = dk_h if dk is None else dk + dk_h
            dv = dv_h if dv is None else dv + dv_h
        sums[g, 0, keys, :] += dk
        sums[g, 1, keys, :] += dv

    def key_block(g, j, in_rim):
        keys = at(j * BLOCK, BLOCK)
        k_turned[:, keys] = k_ext[g, keys, :].astype(jnp.float32).T.astype(jnp.bfloat16)
        sums[g, :, keys, :] = jnp.zeros((2, BLOCK, HEAD_DIM), jnp.float32)
        low, high = jnp.maximum(j - rim_blocks, 0), jnp.minimum(j + 1, q_blocks)
        lax.fori_loop(low, high, lambda i, _: (tile(g, j, i, in_rim), 0)[1], 0)

    def prepare(g):
        ones = jnp.ones((8, HEAD_DIM), jnp.bfloat16)
        for h in range(ratio):
            lanes = slice(h * HEAD_DIM, (h + 1) * HEAD_DIM)
            stats[h : h + 1, :] = norm[pl.ds(g * ratio + h, 1), :] * LOG2E

            def rows_of(i, _, h=h, lanes=lanes):
                rows = at(i * BLOCK, BLOCK)
                both = g_buf[g, rows, lanes].astype(jnp.float32) * o_buf[g, rows, lanes].astype(
                    jnp.float32
                )
                high = both.astype(jnp.bfloat16)
                low = (both - high.astype(jnp.float32)).astype(jnp.bfloat16)
                delta = dot(ones, high, ((1,), (1,))) + dot(ones, low, ((1,), (1,)))
                stats[ratio + h : ratio + h + 1, rows] = delta[0:1, :]
                return 0

            lax.fori_loop(0, q_blocks, rows_of, 0)
            dq_turned[h] = jnp.zeros((HEAD_DIM, tokens), jnp.float32)

    def finish_dq(g):
        def rows_of(i, _):
            rows = at(i * BLOCK, BLOCK)
            for h in range(ratio):
                lanes = slice(h * HEAD_DIM, (h + 1) * HEAD_DIM)
                dq_buf[g, rows, lanes] = (dq_turned[h, :, rows].T * score_scale).astype(
                    jnp.bfloat16
                )
            return 0

        lax.fori_loop(0, q_blocks, rows_of, 0)
        for n in range(heads - 1):
            dq_out(g, n).start()
        dq_own(g).start()

    def finish_dkv(g):
        @pl.when(has_after)
        def _():
            rim_out(g).wait_recv()

            def add(i, _):
                rows = at(i * BLOCK, BLOCK)
                own = at(tokens + i * BLOCK, BLOCK)
                for c in range(2):
                    sums[g, c, own, :] += rims[g, c, rows, :]
                return 0

            lax.fori_loop(0, rim_blocks, add, 0)

        def owner_of(n, _):
            own = at(WINDOW + n * owned, owned)
            dkv_buf[g, n, 0] = (sums[g, 0, own, :] * score_scale).astype(jnp.bfloat16)
            dkv_buf[g, n, 1] = sums[g, 1, own, :].astype(jnp.bfloat16)
            return 0

        lax.fori_loop(0, heads, owner_of, 0)
        for n in range(heads - 1):
            dkv_out(g, n).start()
        dkv_own(g).start()

    barrier = pltpu.get_barrier_semaphore()
    for d in range(1, heads):
        pl.semaphore_signal(
            barrier, inc=1, device_id={"head": lax.rem(z + d, heads)}, device_id_type=MESH
        )

    @pl.when(has_before)
    def _():
        pl.semaphore_signal(barrier, inc=1, device_id={"seq": s - 1}, device_id_type=MESH)

    @pl.when(has_after)
    def _():
        pl.semaphore_signal(barrier, inc=1, device_id={"seq": s + 1}, device_id_type=MESH)

    def start_stage(g, _):
        for n in range(heads - 1):
            stage(g, n).start()
        return 0

    lax.fori_loop(0, groups, start_stage, 0)
    norm_in = pltpu.make_async_copy(n_hbm, norm, norm_sem)
    norm_in.start()
    for copy in inputs(0):
        copy.start()

    pl.semaphore_wait(
        barrier, heads - 1 + has_before.astype(jnp.int32) + has_after.astype(jnp.int32)
    )

    for g in range(min(AHEAD, groups)):
        send_grads(g)
        send_windows(g)
    norm_in.wait()

    def one_group(g, _):
        @pl.when(g + 1 < groups)
        def _():
            for copy in inputs(g + 1):
                copy.start()

        for copy in inputs(g):
            copy.wait()
        for n in range(heads - 1):
            grad_in(g, n, peers[n]).wait_recv()

        @pl.when(g + AHEAD < groups)
        def _():
            send_grads(g + AHEAD)
            send_windows(g + AHEAD)

        prepare(g)

        @pl.when(has_before)
        def _():
            for c in range(2):
                window_in(g, c).wait_recv()
            lax.fori_loop(0, rim_blocks, lambda j, _: (key_block(g, j, True), 0)[1], 0)
            rim_out(g).start()

        @pl.when(g > 0)
        def _():
            finish_dkv(g - 1)

        lax.fori_loop(
            rim_blocks, rim_blocks + q_blocks, lambda j, _: (key_block(g, j, False), 0)[1], 0
        )
        finish_dq(g)
        return 0

    lax.fori_loop(0, groups, one_group, 0)
    finish_dkv(groups - 1)

    def drain(g, _):
        for n in range(heads - 1):
            grad_in(g, n).wait_send()
            dq_out(g, n, peers[n]).wait()
            dkv_out(g, n, peers[n]).wait()
        dq_own(g).wait()
        dkv_own(g).wait()

        @pl.when(has_after)
        def _():
            for c in range(2):
                window_in(g, c).wait_send()

        @pl.when(has_before)
        def _():
            rim_out(g).wait_send()

        return 0

    lax.fori_loop(0, groups, drain, 0)


def write_out(dq_land, dkv_land, dq_hbm, dk_hbm, dv_hbm, sem):
    blocks, _, pair = dq_land.shape

    def copies(n):
        narrow = at(n * HEAD_DIM, HEAD_DIM)
        return [
            pltpu.make_async_copy(dq_land.at[n], dq_hbm.at[:, at(n * pair, pair)], sem.at[n, 0]),
            pltpu.make_async_copy(dkv_land.at[n, 0], dk_hbm.at[:, narrow], sem.at[n, 1]),
            pltpu.make_async_copy(dkv_land.at[n, 1], dv_hbm.at[:, narrow], sem.at[n, 2]),
        ]

    for n in range(blocks):
        for copy in copies(n):
            copy.start()
    for n in range(blocks):
        for copy in copies(n):
            copy.wait()


def on_device(seqs, heads, queries, key_states, value_states, outputs, out_grad, log_norm):
    tokens = queries.shape[0]
    groups = key_states.shape[1] // HEAD_DIM
    ratio = queries.shape[1] // key_states.shape[1]
    pair, owned, span = ratio * HEAD_DIM, tokens // heads, WINDOW + tokens
    low, wide = jnp.bfloat16, jnp.float32
    dma = pltpu.SemaphoreType.DMA
    pairs = groups * ratio * tokens * (WINDOW + BLOCK)
    shapes = [
        (owned, out_grad.shape[1]),
        (owned, key_states.shape[1] * heads),
        (owned, key_states.shape[1] * heads),
    ]
    landed = pl.pallas_call(
        functools.partial(kernel, seqs, heads, groups, ratio, tokens),
        out_shape=[
            pltpu.VMEM((heads * groups, owned, pair), low),
            pltpu.VMEM((heads * groups, 2, owned, HEAD_DIM), low),
        ],
        in_specs=[pl.BlockSpec(memory_space=pltpu.HBM)] * 6,
        out_specs=[pl.BlockSpec(memory_space=pltpu.VMEM)] * 2,
        scratch_shapes=[
            pltpu.VMEM((groups, tokens, pair), low),
            pltpu.VMEM((groups, tokens, pair), low),
            pltpu.VMEM((groups, tokens, pair), low),
            pltpu.VMEM((groups, span, HEAD_DIM), low),
            pltpu.VMEM((groups, span, HEAD_DIM), low),
            pltpu.VMEM(log_norm.shape, wide),
            pltpu.VMEM((2 * ratio, tokens), wide),
            pltpu.VMEM((HEAD_DIM, span), low),
            pltpu.VMEM((ratio, HEAD_DIM, tokens), wide),
            pltpu.VMEM((groups, 2, span, HEAD_DIM), wide),
            pltpu.VMEM((groups, 2, WINDOW, HEAD_DIM), wide),
            pltpu.VMEM((groups, tokens, pair), low),
            pltpu.VMEM((groups, heads, 2, owned, HEAD_DIM), low),
            pltpu.VMEM((groups, heads - 1, owned, pair), low),
            dma((groups, 5)),
            dma,
            dma((groups, heads)),
            dma((groups, heads)),
            dma((groups, heads)),
            dma((groups, 2)),
            dma((groups, 2)),
            dma((groups,)),
            dma((groups,)),
            dma((groups, heads)),
            dma((groups, heads)),
            dma((groups, heads)),
            dma((groups, heads)),
        ],
        cost_estimate=pl.CostEstimate(
            flops=10 * pairs * HEAD_DIM, bytes_accessed=12 * tokens * 1024, transcendentals=pairs
        ),
        compiler_params=pltpu.CompilerParams(
            collective_id=0, has_side_effects=True, vmem_limit_bytes=52 * 1024 * 1024
        ),
    )(queries, key_states, value_states, outputs, out_grad, log_norm)
    return pl.pallas_call(
        write_out,
        out_shape=[jax.ShapeDtypeStruct(shape, low) for shape in shapes],
        in_specs=[pl.BlockSpec(memory_space=pl.ANY)] * 2,
        out_specs=[pl.BlockSpec(memory_space=pltpu.HBM)] * 3,
        scratch_shapes=[dma((heads * groups, 3))],
        compiler_params=pltpu.CompilerParams(vmem_limit_bytes=1024 * 1024),
    )(*landed)


def solution(mesh):
    placed = (
        P("seq", "head"),
        P("seq", "head"),
        P("seq", "head"),
        P("seq", "head"),
        P(("seq", "head"), None),
        P("head", "seq"),
    )
    return jax.shard_map(
        functools.partial(on_device, mesh.shape["seq"], mesh.shape["head"]),
        mesh=mesh,
        in_specs=placed,
        out_specs=(P(("seq", "head"), None), P(("seq", "head"), None), P(("seq", "head"), None)),
        check_vma=False,
    )
```

```python
import functools
import math

import jax
import jax.numpy as jnp
from jax import lax
from jax.experimental import pallas as pl
from jax.experimental.pallas import tpu as pltpu
from jax.sharding import PartitionSpec as P

HEAD_DIM = 128
WINDOW = 1024
BLOCK = 256
AHEAD = 3

score_scale = 168.0 ** (-0.5)
LOG2E = math.log2(math.e)
MESH = pl.DeviceIdType.MESH


def at(start, size, step=None):
    return pl.ds(pl.multiple_of(start, size if step is None else step), size)


def dot(a, b, dims):
    return lax.dot_general(a, b, (dims, ((), ())), preferred_element_type=jnp.float32)


def kernel(
    seqs, heads, groups, ratio, tokens,
    q_hbm, k_hbm, v_hbm, o_hbm, g_hbm, n_hbm,
    dq_land, dkv_land,
    q_buf, o_buf, g_buf, k_ext, v_ext, norm, stats, k_turned, dq_turned,
    sums, rim_low, rims, dq_buf, dkv_buf, staged,
    in_sem, norm_sem, stage_sem, g_send, g_recv, kv_send, kv_recv, rim_send, rim_recv,
    dq_send, dq_recv, dkv_send, dkv_recv,
):
    s, z = lax.axis_index("seq"), lax.axis_index("head")
    owned = tokens // heads
    pair = ratio * HEAD_DIM
    q_blocks, rim_blocks = tokens // BLOCK, WINDOW // BLOCK
    has_before, has_after = s > 0, s < seqs - 1

    half = heads // 2
    in_low = (z < half).astype(jnp.int32)

    def peer_of(n):
        if heads % 2:
            return lax.rem(z + 1 + n, heads)
        if n < half:
            down = heads - 1 - lax.rem(z + n, half)
            up = lax.rem(heads - 1 - z + n, half)
        else:
            down = lax.rem(z + 1 + n - half, half)
            up = half + lax.rem(z + 1 + n - half, half)
        return in_low * down + (1 - in_low) * up

    peers = [peer_of(n) for n in range(heads - 1)]
    mine = heads - 1

    def inputs(g):
        wide, narrow = at(g * pair, pair), at(g * HEAD_DIM, HEAD_DIM)
        own = pl.ds(WINDOW, tokens)
        return [
            pltpu.make_async_copy(q_hbm.at[:, wide], q_buf.at[g], in_sem.at[g, 0]),
            pltpu.make_async_copy(o_hbm.at[:, wide], o_buf.at[g], in_sem.at[g, 1]),
            pltpu.make_async_copy(k_hbm.at[:, narrow], k_ext.at[g, own], in_sem.at[g, 2]),
            pltpu.make_async_copy(v_hbm.at[:, narrow], v_ext.at[g, own], in_sem.at[g, 3]),
            pltpu.make_async_copy(
                g_hbm.at[:, at(z * groups * pair + g * pair, pair)],
                g_buf.at[g, at(z * owned, owned)],
                in_sem.at[g, 4],
            ),
        ]

    def stage(g, n):
        return pltpu.make_async_copy(
            g_hbm.at[:, at(peers[n] * groups * pair + g * pair, pair)],
            staged.at[g, n],
            stage_sem.at[g, n],
        )

    def grad_in(g, n, source=None):
        return pltpu.make_async_remote_copy(
            src_ref=staged.at[g, n],
            dst_ref=g_buf.at[g, at(z * owned, owned)],
            send_sem=g_send.at[g, n],
            recv_sem=g_recv.at[g, z if source is None else source],
            device_id={"head": peers[n]},
            device_id_type=MESH,
        )

    def window_in(g, c):
        src, dst = ((k_hbm, k_ext), (v_hbm, v_ext))[c]
        return pltpu.make_async_remote_copy(
            src_ref=src.at[pl.ds(tokens - WINDOW, WINDOW), at(g * HEAD_DIM, HEAD_DIM)],
            dst_ref=dst.at[g, pl.ds(0, WINDOW)],
            send_sem=kv_send.at[g, c],
            recv_sem=kv_recv.at[g, c],
            device_id={"seq": s + 1},
            device_id_type=MESH,
        )

    def rim_out(g):
        return pltpu.make_async_remote_copy(
            src_ref=rim_low.at[g],
            dst_ref=rims.at[g],
            send_sem=rim_send.at[g],
            recv_sem=rim_recv.at[g],
            device_id={"seq": s - 1},
            device_id_type=MESH,
        )

    def dq_out(g, n, source=None):
        return pltpu.make_async_remote_copy(
            src_ref=dq_buf.at[g, at(peers[n] * owned, owned)],
            dst_ref=dq_land.at[z * groups + g],
            send_sem=dq_send.at[g, n],
            recv_sem=dq_recv.at[g, z if source is None else source],
            device_id={"head": peers[n]},
            device_id_type=MESH,
        )

    def dq_own(g):
        return pltpu.make_async_copy(
            dq_buf.at[g, at(z * owned, owned)], dq_land.at[z * groups + g], dq_send.at[g, mine]
        )

    def dkv_out(g, n, source=None):
        return pltpu.make_async_remote_copy(
            src_ref=dkv_buf.at[g, peers[n]],
            dst_ref=dkv_land.at[z * groups + g],
            send_sem=dkv_send.at[g, n],
            recv_sem=dkv_recv.at[g, z if source is None else source],
            device_id={"head": peers[n]},
            device_id_type=MESH,
        )

    def dkv_own(g):
        return pltpu.make_async_copy(
            dkv_buf.at[g, z], dkv_land.at[z * groups + g], dkv_send.at[g, mine]
        )

    def send_grads(g):
        for n in range(heads - 1):
            stage(g, n).wait()
            grad_in(g, n).start()

    def send_windows(g):
        @pl.when(has_after)
        def _():
            for c in range(2):
                window_in(g, c).start()

    def tile(g, j, i, in_rim):
        keys, rows = at(j * BLOCK, BLOCK), at(i * BLOCK, BLOCK)
        k_rows, v_rows, k_cols = k_ext[g, keys, :], v_ext[g, keys, :], k_turned[:, keys]
        ahead = lax.broadcasted_iota(jnp.int32, (BLOCK, BLOCK), 1) - lax.broadcasted_iota(
            jnp.int32, (BLOCK, BLOCK), 0
        )
        allowed = None
        if in_rim or q_blocks > rim_blocks:
            allowed = ahead < jnp.where(i < j, BLOCK, 0)
        if not in_rim:
            later = ahead >= jnp.where(i > j - rim_blocks, -BLOCK, 0)
            allowed = later if allowed is None else allowed & later
        dk = dv = None
        for h in range(ratio):
            lanes = slice(h * HEAD_DIM, (h + 1) * HEAD_DIM)
            q_rows, g_rows = q_buf[g, rows, lanes], g_buf[g, rows, lanes]
            scores = dot(k_rows, q_rows, ((1,), (1,)))
            probs = jnp.exp2(scores * (score_scale * LOG2E) - stats[h : h + 1, rows])
            probs = jnp.where(allowed, probs, 0.0)
            grad_prob = dot(v_rows, g_rows, ((1,), (1,)))
            grad_score = (
                probs * (grad_prob - stats[ratio + h : ratio + h + 1, rows])
            ).astype(jnp.bfloat16)
            dv_h = dot(probs.astype(jnp.bfloat16), g_rows, ((1,), (0,)))
            dk_h = dot(grad_score, q_rows, ((1,), (0,)))
            dq_turned[h, :, rows] += dot(k_cols, grad_score, ((1,), (0,)))
            dk = dk_h if dk is None else dk + dk_h
            dv = dv_h if dv is None else dv + dv_h
        sums[g, 0, keys, :] += dk
        sums[g, 1, keys, :] += dv

    def key_block(g, j, in_rim):
        keys = at(j * BLOCK, BLOCK)
        k_turned[:, keys] = k_ext[g, keys, :].astype(jnp.float32).T.astype(jnp.bfloat16)
        sums[g, :, keys, :] = jnp.zeros((2, BLOCK, HEAD_DIM), jnp.float32)
        low, high = jnp.maximum(j - rim_blocks, 0), jnp.minimum(j + 1, q_blocks)
        lax.fori_loop(low, high, lambda i, _: (tile(g, j, i, in_rim), 0)[1], 0)
        if in_rim:
            rim_low[g, :, keys, :] = sums[g, :, keys, :].astype(jnp.bfloat16)

    def prepare(g):
        ones = jnp.ones((8, HEAD_DIM), jnp.bfloat16)
        for h in range(ratio):
            lanes = slice(h * HEAD_DIM, (h + 1) * HEAD_DIM)
            stats[h : h + 1, :] = norm[pl.ds(g * ratio + h, 1), :] * LOG2E

            def rows_of(i, _, h=h, lanes=lanes):
                rows = at(i * BLOCK, BLOCK)
                both = g_buf[g, rows, lanes].astype(jnp.float32) * o_buf[g, rows, lanes].astype(
                    jnp.float32
                )
                high = both.astype(jnp.bfloat16)
                low = (both - high.astype(jnp.float32)).astype(jnp.bfloat16)
                delta = dot(ones, high, ((1,), (1,))) + dot(ones, low, ((1,), (1,)))
                stats[ratio + h : ratio + h + 1, rows] = delta[0:1, :]
                return 0

            lax.fori_loop(0, q_blocks, rows_of, 0)
            dq_turned[h] = jnp.zeros((HEAD_DIM, tokens), jnp.float32)

    def finish_dq(g):
        def rows_of(i, _):
            rows = at(i * BLOCK, BLOCK)
            for h in range(ratio):
                lanes = slice(h * HEAD_DIM, (h + 1) * HEAD_DIM)
                dq_buf[g, rows, lanes] = (dq_turned[h, :, rows].T * score_scale).astype(
                    jnp.bfloat16
                )
            return 0

        lax.fori_loop(0, q_blocks, rows_of, 0)
        for n in range(heads - 1):
            dq_out(g, n).start()
        dq_own(g).start()

    def finish_dkv(g):
        @pl.when(has_after)
        def _():
            rim_out(g).wait_recv()

            def add(i, _):
                rows = at(i * BLOCK, BLOCK)
                own = at(tokens + i * BLOCK, BLOCK)
                for c in range(2):
                    sums[g, c, own, :] += rims[g, c, rows, :].astype(jnp.float32)
                return 0

            lax.fori_loop(0, rim_blocks, add, 0)

        def owner_of(n, _):
            own = at(WINDOW + n * owned, owned)
            dkv_buf[g, n, 0] = (sums[g, 0, own, :] * score_scale).astype(jnp.bfloat16)
            dkv_buf[g, n, 1] = sums[g, 1, own, :].astype(jnp.bfloat16)
            return 0

        lax.fori_loop(0, heads, owner_of, 0)
        for n in range(heads - 1):
            dkv_out(g, n).start()
        dkv_own(g).start()

    barrier = pltpu.get_barrier_semaphore()
    for d in range(1, heads):
        pl.semaphore_signal(
            barrier, inc=1, device_id={"head": lax.rem(z + d, heads)}, device_id_type=MESH
        )

    @pl.when(has_before)
    def _():
        pl.semaphore_signal(barrier, inc=1, device_id={"seq": s - 1}, device_id_type=MESH)

    @pl.when(has_after)
    def _():
        pl.semaphore_signal(barrier, inc=1, device_id={"seq": s + 1}, device_id_type=MESH)

    def start_stage(g, _):
        for n in range(heads - 1):
            stage(g, n).start()
        return 0

    lax.fori_loop(0, groups, start_stage, 0)
    norm_in = pltpu.make_async_copy(n_hbm, norm, norm_sem)
    norm_in.start()
    for copy in inputs(0):
        copy.start()

    pl.semaphore_wait(
        barrier, heads - 1 + has_before.astype(jnp.int32) + has_after.astype(jnp.int32)
    )

    for g in range(min(AHEAD, groups)):
        send_grads(g)
        send_windows(g)
    norm_in.wait()

    def one_group(g, _):
        @pl.when(g + 1 < groups)
        def _():
            for copy in inputs(g + 1):
                copy.start()

        for copy in inputs(g):
            copy.wait()
        for n in range(heads - 1):
            grad_in(g, n, peers[n]).wait_recv()

        @pl.when(g + AHEAD < groups)
        def _():
            send_grads(g + AHEAD)
            send_windows(g + AHEAD)

        prepare(g)

        @pl.when(has_before)
        def _():
            for c in range(2):
                window_in(g, c).wait_recv()
            lax.fori_loop(0, rim_blocks, lambda j, _: (key_block(g, j, True), 0)[1], 0)
            rim_out(g).start()

        @pl.when(g > 0)
        def _():
            finish_dkv(g - 1)

        lax.fori_loop(
            rim_blocks, rim_blocks + q_blocks, lambda j, _: (key_block(g, j, False), 0)[1], 0
        )
        finish_dq(g)
        return 0

    lax.fori_loop(0, groups, one_group, 0)
    finish_dkv(groups - 1)

    def drain(g, _):
        for n in range(heads - 1):
            grad_in(g, n).wait_send()
            dq_out(g, n, peers[n]).wait()
            dkv_out(g, n, peers[n]).wait()
        dq_own(g).wait()
        dkv_own(g).wait()

        @pl.when(has_after)
        def _():
            for c in range(2):
                window_in(g, c).wait_send()

        @pl.when(has_before)
        def _():
            rim_out(g).wait_send()

        return 0

    lax.fori_loop(0, groups, drain, 0)


def write_out(dq_land, dkv_land, dq_hbm, dk_hbm, dv_hbm, sem):
    blocks, _, pair = dq_land.shape

    def copies(n):
        narrow = at(n * HEAD_DIM, HEAD_DIM)
        return [
            pltpu.make_async_copy(dq_land.at[n], dq_hbm.at[:, at(n * pair, pair)], sem.at[n, 0]),
            pltpu.make_async_copy(dkv_land.at[n, 0], dk_hbm.at[:, narrow], sem.at[n, 1]),
            pltpu.make_async_copy(dkv_land.at[n, 1], dv_hbm.at[:, narrow], sem.at[n, 2]),
        ]

    for n in range(blocks):
        for copy in copies(n):
            copy.start()
    for n in range(blocks):
        for copy in copies(n):
            copy.wait()


def on_device(seqs, heads, queries, key_states, value_states, outputs, out_grad, log_norm):
    tokens = queries.shape[0]
    groups = key_states.shape[1] // HEAD_DIM
    ratio = queries.shape[1] // key_states.shape[1]
    pair, owned, span = ratio * HEAD_DIM, tokens // heads, WINDOW + tokens
    low, wide = jnp.bfloat16, jnp.float32
    dma = pltpu.SemaphoreType.DMA
    pairs = groups * ratio * tokens * (WINDOW + BLOCK)
    shapes = [
        (owned, out_grad.shape[1]),
        (owned, key_states.shape[1] * heads),
        (owned, key_states.shape[1] * heads),
    ]
    landed = pl.pallas_call(
        functools.partial(kernel, seqs, heads, groups, ratio, tokens),
        out_shape=[
            pltpu.VMEM((heads * groups, owned, pair), low),
            pltpu.VMEM((heads * groups, 2, owned, HEAD_DIM), low),
        ],
        in_specs=[pl.BlockSpec(memory_space=pltpu.HBM)] * 6,
        out_specs=[pl.BlockSpec(memory_space=pltpu.VMEM)] * 2,
        scratch_shapes=[
            pltpu.VMEM((groups, tokens, pair), low),
            pltpu.VMEM((groups, tokens, pair), low),
            pltpu.VMEM((groups, tokens, pair), low),
            pltpu.VMEM((groups, span, HEAD_DIM), low),
            pltpu.VMEM((groups, span, HEAD_DIM), low),
            pltpu.VMEM(log_norm.shape, wide),
            pltpu.VMEM((2 * ratio, tokens), wide),
            pltpu.VMEM((HEAD_DIM, span), low),
            pltpu.VMEM((ratio, HEAD_DIM, tokens), wide),
            pltpu.VMEM((groups, 2, span, HEAD_DIM), wide),
            pltpu.VMEM((groups, 2, WINDOW, HEAD_DIM), low),
            pltpu.VMEM((groups, 2, WINDOW, HEAD_DIM), low),
            pltpu.VMEM((groups, tokens, pair), low),
            pltpu.VMEM((groups, heads, 2, owned, HEAD_DIM), low),
            pltpu.VMEM((groups, heads - 1, owned, pair), low),
            dma((groups, 5)),
            dma,
            dma((groups, heads)),
            dma((groups, heads)),
            dma((groups, heads)),
            dma((groups, 2)),
            dma((groups, 2)),
            dma((groups,)),
            dma((groups,)),
            dma((groups, heads)),
            dma((groups, heads)),
            dma((groups, heads)),
            dma((groups, heads)),
        ],
        cost_estimate=pl.CostEstimate(
            flops=10 * pairs * HEAD_DIM, bytes_accessed=12 * tokens * 1024, transcendentals=pairs
        ),
        compiler_params=pltpu.CompilerParams(
            collective_id=0, has_side_effects=True, vmem_limit_bytes=52 * 1024 * 1024
        ),
    )(queries, key_states, value_states, outputs, out_grad, log_norm)
    return pl.pallas_call(
        write_out,
        out_shape=[jax.ShapeDtypeStruct(shape, low) for shape in shapes],
        in_specs=[pl.BlockSpec(memory_space=pl.ANY)] * 2,
        out_specs=[pl.BlockSpec(memory_space=pltpu.HBM)] * 3,
        scratch_shapes=[dma((heads * groups, 3))],
        compiler_params=pltpu.CompilerParams(vmem_limit_bytes=1024 * 1024),
    )(*landed)


def solution(mesh):
    placed = (
        P("seq", "head"),
        P("seq", "head"),
        P("seq", "head"),
        P("seq", "head"),
        P(("seq", "head"), None),
        P("head", "seq"),
    )
    return jax.shard_map(
        functools.partial(on_device, mesh.shape["seq"], mesh.shape["head"]),
        mesh=mesh,
        in_specs=placed,
        out_specs=(P(("seq", "head"), None), P(("seq", "head"), None), P(("seq", "head"), None)),
        check_vma=False,
    )
```

```python
import functools
import math

import jax
import jax.numpy as jnp
from jax import lax
from jax.experimental import pallas as pl
from jax.experimental.pallas import tpu as pltpu
from jax.sharding import PartitionSpec as P

HEAD_DIM = 128
WINDOW = 1024
BLOCK = 256
AHEAD = 3

score_scale = 168.0 ** (-0.5)
LOG2E = math.log2(math.e)
MESH = pl.DeviceIdType.MESH


def at(start, size, step=None):
    return pl.ds(pl.multiple_of(start, size if step is None else step), size)


def dot(a, b, dims):
    return lax.dot_general(a, b, (dims, ((), ())), preferred_element_type=jnp.float32)


def kernel(
    seqs, heads, groups, ratio, tokens,
    q_hbm, k_hbm, v_hbm, o_hbm, g_hbm, n_hbm,
    dq_land, dkv_land,
    q_buf, o_buf, g_buf, k_ext, v_ext, norm, stats, k_turned, dq_turned,
    sums, rims, dq_buf, dkv_buf, staged,
    in_sem, norm_sem, stage_sem, g_send, g_recv, kv_send, kv_recv, rim_send, rim_recv,
    dq_send, dq_recv, dkv_send, dkv_recv,
):
    s, z = lax.axis_index("seq"), lax.axis_index("head")
    owned = tokens // heads
    pair = ratio * HEAD_DIM
    q_blocks, rim_blocks = tokens // BLOCK, WINDOW // BLOCK
    has_before, has_after = s > 0, s < seqs - 1

    half, edge = heads // 2, heads // 4
    in_low = (z < half).astype(jnp.int32)
    inner = (z >= edge).astype(jnp.int32) * (z < heads - edge).astype(jnp.int32)

    def same_half(n):
        return (1 - in_low) * half + lax.rem(z + 1 + n, half)

    def peer_of(n):
        if heads % 2:
            return lax.rem(z + 1 + n, heads)
        if n < half:
            from_edge = in_low * (half + n) + (1 - in_low) * (half - 1 - n)
        else:
            from_edge = same_half(n - half)
        if n < half - 1:
            from_inner = same_half(n)
        else:
            far = n - (half - 1)
            from_inner = in_low * (heads - 1 - far) + (1 - in_low) * far
        return inner * from_inner + (1 - inner) * from_edge

    peers = [peer_of(n) for n in range(heads - 1)]
    mine = heads - 1

    def inputs(g):
        wide, narrow = at(g * pair, pair), at(g * HEAD_DIM, HEAD_DIM)
        own = pl.ds(WINDOW, tokens)
        return [
            pltpu.make_async_copy(q_hbm.at[:, wide], q_buf.at[g], in_sem.at[g, 0]),
            pltpu.make_async_copy(o_hbm.at[:, wide], o_buf.at[g], in_sem.at[g, 1]),
            pltpu.make_async_copy(k_hbm.at[:, narrow], k_ext.at[g, own], in_sem.at[g, 2]),
            pltpu.make_async_copy(v_hbm.at[:, narrow], v_ext.at[g, own], in_sem.at[g, 3]),
            pltpu.make_async_copy(
                g_hbm.at[:, at(z * groups * pair + g * pair, pair)],
                g_buf.at[g, at(z * owned, owned)],
                in_sem.at[g, 4],
            ),
        ]

    def stage(g, n):
        return pltpu.make_async_copy(
            g_hbm.at[:, at(peers[n] * groups * pair + g * pair, pair)],
            staged.at[g, n],
            stage_sem.at[g, n],
        )

    def grad_in(g, n, source=None):
        return pltpu.make_async_remote_copy(
            src_ref=staged.at[g, n],
            dst_ref=g_buf.at[g, at(z * owned, owned)],
            send_sem=g_send.at[g, n],
            recv_sem=g_recv.at[g, z if source is None else source],
            device_id={"head": peers[n]},
            device_id_type=MESH,
        )

    def window_in(g, c):
        src, dst = ((k_hbm, k_ext), (v_hbm, v_ext))[c]
        return pltpu.make_async_remote_copy(
            src_ref=src.at[pl.ds(tokens - WINDOW, WINDOW), at(g * HEAD_DIM, HEAD_DIM)],
            dst_ref=dst.at[g, pl.ds(0, WINDOW)],
            send_sem=kv_send.at[g, c],
            recv_sem=kv_recv.at[g, c],
            device_id={"seq": s + 1},
            device_id_type=MESH,
        )

    def rim_out(g):
        return pltpu.make_async_remote_copy(
            src_ref=sums.at[g, :, pl.ds(0, WINDOW)],
            dst_ref=rims.at[g],
            send_sem=rim_send.at[g],
            recv_sem=rim_recv.at[g],
            device_id={"seq": s - 1},
            device_id_type=MESH,
        )

    def dq_out(g, n, source=None):
        return pltpu.make_async_remote_copy(
            src_ref=dq_buf.at[g, at(peers[n] * owned, owned)],
            dst_ref=dq_land.at[z * groups + g],
            send_sem=dq_send.at[g, n],
            recv_sem=dq_recv.at[g, z if source is None else source],
            device_id={"head": peers[n]},
            device_id_type=MESH,
        )

    def dq_own(g):
        return pltpu.make_async_copy(
            dq_buf.at[g, at(z * owned, owned)], dq_land.at[z * groups + g], dq_send.at[g, mine]
        )

    def dkv_out(g, n, source=None):
        return pltpu.make_async_remote_copy(
            src_ref=dkv_buf.at[g, peers[n]],
            dst_ref=dkv_land.at[z * groups + g],
            send_sem=dkv_send.at[g, n],
            recv_sem=dkv_recv.at[g, z if source is None else source],
            device_id={"head": peers[n]},
            device_id_type=MESH,
        )

    def dkv_own(g):
        return pltpu.make_async_copy(
            dkv_buf.at[g, z], dkv_land.at[z * groups + g], dkv_send.at[g, mine]
        )

    def send_grads(g):
        for n in range(heads - 1):
            stage(g, n).wait()
            grad_in(g, n).start()

    def send_windows(g):
        @pl.when(has_after)
        def _():
            for c in range(2):
                window_in(g, c).start()

    def tile(g, j, i, in_rim):
        keys, rows = at(j * BLOCK, BLOCK), at(i * BLOCK, BLOCK)
        k_rows, v_rows, k_cols = k_ext[g, keys, :], v_ext[g, keys, :], k_turned[:, keys]
        ahead = lax.broadcasted_iota(jnp.int32, (BLOCK, BLOCK), 1) - lax.broadcasted_iota(
            jnp.int32, (BLOCK, BLOCK), 0
        )
        allowed = None
        if in_rim or q_blocks > rim_blocks:
            allowed = ahead < jnp.where(i < j, BLOCK, 0)
        if not in_rim:
            later = ahead >= jnp.where(i > j - rim_blocks, -BLOCK, 0)
            allowed = later if allowed is None else allowed & later
        dk = dv = None
        for h in range(ratio):
            lanes = slice(h * HEAD_DIM, (h + 1) * HEAD_DIM)
            q_rows, g_rows = q_buf[g, rows, lanes], g_buf[g, rows, lanes]
            scores = dot(k_rows, q_rows, ((1,), (1,)))
            probs = jnp.exp2(scores * (score_scale * LOG2E) - stats[h : h + 1, rows])
            probs = jnp.where(allowed, probs, 0.0)
            grad_prob = dot(v_rows, g_rows, ((1,), (1,)))
            grad_score = (
                probs * (grad_prob - stats[ratio + h : ratio + h + 1, rows])
            ).astype(jnp.bfloat16)
            dv_h = dot(probs.astype(jnp.bfloat16), g_rows, ((1,), (0,)))
            dk_h = dot(grad_score, q_rows, ((1,), (0,)))
            dq_turned[h, :, rows] += dot(k_cols, grad_score, ((1,), (0,)))
            dk = dk_h if dk is None else dk + dk_h
            dv = dv_h if dv is None else dv + dv_h
        sums[g, 0, keys, :] += dk
        sums[g, 1, keys, :] += dv

    def key_block(g, j, in_rim):
        keys = at(j * BLOCK, BLOCK)
        k_turned[:, keys] = k_ext[g, keys, :].astype(jnp.float32).T.astype(jnp.bfloat16)
        sums[g, :, keys, :] = jnp.zeros((2, BLOCK, HEAD_DIM), jnp.float32)
        low, high = jnp.maximum(j - rim_blocks, 0), jnp.minimum(j + 1, q_blocks)
        lax.fori_loop(low, high, lambda i, _: (tile(g, j, i, in_rim), 0)[1], 0)

    def prepare(g):
        ones = jnp.ones((8, HEAD_DIM), jnp.bfloat16)
        for h in range(ratio):
            lanes = slice(h * HEAD_DIM, (h + 1) * HEAD_DIM)
            stats[h : h + 1, :] = norm[pl.ds(g * ratio + h, 1), :] * LOG2E

            def rows_of(i, _, h=h, lanes=lanes):
                rows = at(i * BLOCK, BLOCK)
                both = g_buf[g, rows, lanes].astype(jnp.float32) * o_buf[g, rows, lanes].astype(
                    jnp.float32
                )
                high = both.astype(jnp.bfloat16)
                low = (both - high.astype(jnp.float32)).astype(jnp.bfloat16)
                delta = dot(ones, high, ((1,), (1,))) + dot(ones, low, ((1,), (1,)))
                stats[ratio + h : ratio + h + 1, rows] = delta[0:1, :]
                return 0

            lax.fori_loop(0, q_blocks, rows_of, 0)
            dq_turned[h] = jnp.zeros((HEAD_DIM, tokens), jnp.float32)

    def finish_dq(g):
        def rows_of(i, _):
            rows = at(i * BLOCK, BLOCK)
            for h in range(ratio):
                lanes = slice(h * HEAD_DIM, (h + 1) * HEAD_DIM)
                dq_buf[g, rows, lanes] = (dq_turned[h, :, rows].T * score_scale).astype(
                    jnp.bfloat16
                )
            return 0

        lax.fori_loop(0, q_blocks, rows_of, 0)
        for n in range(heads - 1):
            dq_out(g, n).start()
        dq_own(g).start()

    def finish_dkv(g):
        @pl.when(has_after)
        def _():
            rim_out(g).wait_recv()

            def add(i, _):
                rows = at(i * BLOCK, BLOCK)
                own = at(tokens + i * BLOCK, BLOCK)
                for c in range(2):
                    sums[g, c, own, :] += rims[g, c, rows, :]
                return 0

            lax.fori_loop(0, rim_blocks, add, 0)

        def owner_of(n, _):
            own = at(WINDOW + n * owned, owned)
            dkv_buf[g, n, 0] = (sums[g, 0, own, :] * score_scale).astype(jnp.bfloat16)
            dkv_buf[g, n, 1] = sums[g, 1, own, :].astype(jnp.bfloat16)
            return 0

        lax.fori_loop(0, heads, owner_of, 0)
        for n in range(heads - 1):
            dkv_out(g, n).start()
        dkv_own(g).start()

    barrier = pltpu.get_barrier_semaphore()
    for d in range(1, heads):
        pl.semaphore_signal(
            barrier, inc=1, device_id={"head": lax.rem(z + d, heads)}, device_id_type=MESH
        )

    @pl.when(has_before)
    def _():
        pl.semaphore_signal(barrier, inc=1, device_id={"seq": s - 1}, device_id_type=MESH)

    @pl.when(has_after)
    def _():
        pl.semaphore_signal(barrier, inc=1, device_id={"seq": s + 1}, device_id_type=MESH)

    def start_stage(g, _):
        for n in range(heads - 1):
            stage(g, n).start()
        return 0

    lax.fori_loop(0, groups, start_stage, 0)
    norm_in = pltpu.make_async_copy(n_hbm, norm, norm_sem)
    norm_in.start()
    for copy in inputs(0):
        copy.start()

    pl.semaphore_wait(
        barrier, heads - 1 + has_before.astype(jnp.int32) + has_after.astype(jnp.int32)
    )

    for g in range(min(AHEAD, groups)):
        send_grads(g)
        send_windows(g)
    norm_in.wait()

    def one_group(g, _):
        @pl.when(g + 1 < groups)
        def _():
            for copy in inputs(g + 1):
                copy.start()

        for copy in inputs(g):
            copy.wait()
        for n in range(heads - 1):
            grad_in(g, n, peers[n]).wait_recv()

        @pl.when(g + AHEAD < groups)
        def _():
            send_grads(g + AHEAD)
            send_windows(g + AHEAD)

        prepare(g)

        @pl.when(has_before)
        def _():
            for c in range(2):
                window_in(g, c).wait_recv()
            lax.fori_loop(0, rim_blocks, lambda j, _: (key_block(g, j, True), 0)[1], 0)
            rim_out(g).start()

        @pl.when(g > 0)
        def _():
            finish_dkv(g - 1)

        lax.fori_loop(
            rim_blocks, rim_blocks + q_blocks, lambda j, _: (key_block(g, j, False), 0)[1], 0
        )
        finish_dq(g)
        return 0

    lax.fori_loop(0, groups, one_group, 0)
    finish_dkv(groups - 1)

    def drain(g, _):
        for n in range(heads - 1):
            grad_in(g, n).wait_send()
            dq_out(g, n, peers[n]).wait()
            dkv_out(g, n, peers[n]).wait()
        dq_own(g).wait()
        dkv_own(g).wait()

        @pl.when(has_after)
        def _():
            for c in range(2):
                window_in(g, c).wait_send()

        @pl.when(has_before)
        def _():
            rim_out(g).wait_send()

        return 0

    lax.fori_loop(0, groups, drain, 0)


def write_out(dq_land, dkv_land, dq_hbm, dk_hbm, dv_hbm, sem):
    blocks, _, pair = dq_land.shape

    def copies(n):
        narrow = at(n * HEAD_DIM, HEAD_DIM)
        return [
            pltpu.make_async_copy(dq_land.at[n], dq_hbm.at[:, at(n * pair, pair)], sem.at[n, 0]),
            pltpu.make_async_copy(dkv_land.at[n, 0], dk_hbm.at[:, narrow], sem.at[n, 1]),
            pltpu.make_async_copy(dkv_land.at[n, 1], dv_hbm.at[:, narrow], sem.at[n, 2]),
        ]

    for n in range(blocks):
        for copy in copies(n):
            copy.start()
    for n in range(blocks):
        for copy in copies(n):
            copy.wait()


def on_device(seqs, heads, queries, key_states, value_states, outputs, out_grad, log_norm):
    tokens = queries.shape[0]
    groups = key_states.shape[1] // HEAD_DIM
    ratio = queries.shape[1] // key_states.shape[1]
    pair, owned, span = ratio * HEAD_DIM, tokens // heads, WINDOW + tokens
    low, wide = jnp.bfloat16, jnp.float32
    dma = pltpu.SemaphoreType.DMA
    pairs = groups * ratio * tokens * (WINDOW + BLOCK)
    shapes = [
        (owned, out_grad.shape[1]),
        (owned, key_states.shape[1] * heads),
        (owned, key_states.shape[1] * heads),
    ]
    landed = pl.pallas_call(
        functools.partial(kernel, seqs, heads, groups, ratio, tokens),
        out_shape=[
            pltpu.VMEM((heads * groups, owned, pair), low),
            pltpu.VMEM((heads * groups, 2, owned, HEAD_DIM), low),
        ],
        in_specs=[pl.BlockSpec(memory_space=pltpu.HBM)] * 6,
        out_specs=[pl.BlockSpec(memory_space=pltpu.VMEM)] * 2,
        scratch_shapes=[
            pltpu.VMEM((groups, tokens, pair), low),
            pltpu.VMEM((groups, tokens, pair), low),
            pltpu.VMEM((groups, tokens, pair), low),
            pltpu.VMEM((groups, span, HEAD_DIM), low),
            pltpu.VMEM((groups, span, HEAD_DIM), low),
            pltpu.VMEM(log_norm.shape, wide),
            pltpu.VMEM((2 * ratio, tokens), wide),
            pltpu.VMEM((HEAD_DIM, span), low),
            pltpu.VMEM((ratio, HEAD_DIM, tokens), wide),
            pltpu.VMEM((groups, 2, span, HEAD_DIM), wide),
            pltpu.VMEM((groups, 2, WINDOW, HEAD_DIM), wide),
            pltpu.VMEM((groups, tokens, pair), low),
            pltpu.VMEM((groups, heads, 2, owned, HEAD_DIM), low),
            pltpu.VMEM((groups, heads - 1, owned, pair), low),
            dma((groups, 5)),
            dma,
            dma((groups, heads)),
            dma((groups, heads)),
            dma((groups, heads)),
            dma((groups, 2)),
            dma((groups, 2)),
            dma((groups,)),
            dma((groups,)),
            dma((groups, heads)),
            dma((groups, heads)),
            dma((groups, heads)),
            dma((groups, heads)),
        ],
        cost_estimate=pl.CostEstimate(
            flops=10 * pairs * HEAD_DIM, bytes_accessed=12 * tokens * 1024, transcendentals=pairs
        ),
        compiler_params=pltpu.CompilerParams(
            collective_id=0, has_side_effects=True, vmem_limit_bytes=52 * 1024 * 1024
        ),
    )(queries, key_states, value_states, outputs, out_grad, log_norm)
    return pl.pallas_call(
        write_out,
        out_shape=[jax.ShapeDtypeStruct(shape, low) for shape in shapes],
        in_specs=[pl.BlockSpec(memory_space=pl.ANY)] * 2,
        out_specs=[pl.BlockSpec(memory_space=pltpu.HBM)] * 3,
        scratch_shapes=[dma((heads * groups, 3))],
        compiler_params=pltpu.CompilerParams(vmem_limit_bytes=1024 * 1024),
    )(*landed)


def solution(mesh):
    placed = (
        P("seq", "head"),
        P("seq", "head"),
        P("seq", "head"),
        P("seq", "head"),
        P(("seq", "head"), None),
        P("head", "seq"),
    )
    return jax.shard_map(
        functools.partial(on_device, mesh.shape["seq"], mesh.shape["head"]),
        mesh=mesh,
        in_specs=placed,
        out_specs=(P(("seq", "head"), None), P(("seq", "head"), None), P(("seq", "head"), None)),
        check_vma=False,
    )
```

```python
import functools
import math

import jax
import jax.numpy as jnp
from jax import lax
from jax.experimental import pallas as pl
from jax.experimental.pallas import tpu as pltpu
from jax.sharding import PartitionSpec as P

HEAD_DIM = 128
WINDOW = 1024
BLOCK = 256
AHEAD = 3

score_scale = 168.0 ** (-0.5)
LOG2E = math.log2(math.e)
MESH = pl.DeviceIdType.MESH


def at(start, size, step=None):
    return pl.ds(pl.multiple_of(start, size if step is None else step), size)


def dot(a, b, dims):
    return lax.dot_general(a, b, (dims, ((), ())), preferred_element_type=jnp.float32)


def kernel(
    seqs, heads, groups, ratio, tokens,
    q_hbm, k_hbm, v_hbm, o_hbm, g_hbm, n_hbm,
    dq_land, dkv_land,
    q_buf, o_buf, g_buf, k_ext, v_ext, norm, stats, k_turned, dq_turned,
    sums, rim_low, rims, dq_buf, dkv_buf, staged,
    in_sem, norm_sem, stage_sem, g_send, g_recv, kv_send, kv_recv, rim_send, rim_recv,
    dq_send, dq_recv, dkv_send, dkv_recv,
):
    s, z = lax.axis_index("seq"), lax.axis_index("head")
    owned = tokens // heads
    pair = ratio * HEAD_DIM
    q_blocks, rim_blocks = tokens // BLOCK, WINDOW // BLOCK
    has_before, has_after = s > 0, s < seqs - 1

    half, edge = heads // 2, heads // 4
    in_low = (z < half).astype(jnp.int32)
    inner = (z >= edge).astype(jnp.int32) * (z < heads - edge).astype(jnp.int32)

    def same_half(n):
        return (1 - in_low) * half + lax.rem(z + 1 + n, half)

    def peer_of(n):
        if heads % 2:
            return lax.rem(z + 1 + n, heads)
        if n < half:
            from_edge = in_low * (half + n) + (1 - in_low) * (half - 1 - n)
        else:
            from_edge = same_half(n - half)
        if n < half - 1:
            from_inner = same_half(n)
        else:
            far = n - (half - 1)
            from_inner = in_low * (heads - 1 - far) + (1 - in_low) * far
        return inner * from_inner + (1 - inner) * from_edge

    peers = [peer_of(n) for n in range(heads - 1)]
    mine = heads - 1

    def inputs(g):
        wide, narrow = at(g * pair, pair), at(g * HEAD_DIM, HEAD_DIM)
        own = pl.ds(WINDOW, tokens)
        return [
            pltpu.make_async_copy(q_hbm.at[:, wide], q_buf.at[g], in_sem.at[g, 0]),
            pltpu.make_async_copy(o_hbm.at[:, wide], o_buf.at[g], in_sem.at[g, 1]),
            pltpu.make_async_copy(k_hbm.at[:, narrow], k_ext.at[g, own], in_sem.at[g, 2]),
            pltpu.make_async_copy(v_hbm.at[:, narrow], v_ext.at[g, own], in_sem.at[g, 3]),
            pltpu.make_async_copy(
                g_hbm.at[:, at(z * groups * pair + g * pair, pair)],
                g_buf.at[g, at(z * owned, owned)],
                in_sem.at[g, 4],
            ),
        ]

    def stage(g, n):
        return pltpu.make_async_copy(
            g_hbm.at[:, at(peers[n] * groups * pair + g * pair, pair)],
            staged.at[g, n],
            stage_sem.at[g, n],
        )

    def grad_in(g, n, source=None):
        return pltpu.make_async_remote_copy(
            src_ref=staged.at[g, n],
            dst_ref=g_buf.at[g, at(z * owned, owned)],
            send_sem=g_send.at[g, n],
            recv_sem=g_recv.at[g, z if source is None else source],
            device_id={"head": peers[n]},
            device_id_type=MESH,
        )

    def window_in(g, c):
        src, dst = ((k_hbm, k_ext), (v_hbm, v_ext))[c]
        return pltpu.make_async_remote_copy(
            src_ref=src.at[pl.ds(tokens - WINDOW, WINDOW), at(g * HEAD_DIM, HEAD_DIM)],
            dst_ref=dst.at[g, pl.ds(0, WINDOW)],
            send_sem=kv_send.at[g, c],
            recv_sem=kv_recv.at[g, c],
            device_id={"seq": s + 1},
            device_id_type=MESH,
        )

    def rim_out(g):
        return pltpu.make_async_remote_copy(
            src_ref=rim_low.at[g],
            dst_ref=rims.at[g],
            send_sem=rim_send.at[g],
            recv_sem=rim_recv.at[g],
            device_id={"seq": s - 1},
            device_id_type=MESH,
        )

    def dq_out(g, n, source=None):
        return pltpu.make_async_remote_copy(
            src_ref=dq_buf.at[g, at(peers[n] * owned, owned)],
            dst_ref=dq_land.at[z * groups + g],
            send_sem=dq_send.at[g, n],
            recv_sem=dq_recv.at[g, z if source is None else source],
            device_id={"head": peers[n]},
            device_id_type=MESH,
        )

    def dq_own(g):
        return pltpu.make_async_copy(
            dq_buf.at[g, at(z * owned, owned)], dq_land.at[z * groups + g], dq_send.at[g, mine]
        )

    def dkv_out(g, n, source=None):
        return pltpu.make_async_remote_copy(
            src_ref=dkv_buf.at[g, peers[n]],
            dst_ref=dkv_land.at[z * groups + g],
            send_sem=dkv_send.at[g, n],
            recv_sem=dkv_recv.at[g, z if source is None else source],
            device_id={"head": peers[n]},
            device_id_type=MESH,
        )

    def dkv_own(g):
        return pltpu.make_async_copy(
            dkv_buf.at[g, z], dkv_land.at[z * groups + g], dkv_send.at[g, mine]
        )

    def send_grads(g):
        for n in range(heads - 1):
            stage(g, n).wait()
            grad_in(g, n).start()

    def send_windows(g):
        @pl.when(has_after)
        def _():
            for c in range(2):
                window_in(g, c).start()

    def tile(g, j, i, in_rim):
        keys, rows = at(j * BLOCK, BLOCK), at(i * BLOCK, BLOCK)
        k_rows, v_rows, k_cols = k_ext[g, keys, :], v_ext[g, keys, :], k_turned[:, keys]
        ahead = lax.broadcasted_iota(jnp.int32, (BLOCK, BLOCK), 1) - lax.broadcasted_iota(
            jnp.int32, (BLOCK, BLOCK), 0
        )
        allowed = None
        if in_rim or q_blocks > rim_blocks:
            allowed = ahead < jnp.where(i < j, BLOCK, 0)
        if not in_rim:
            later = ahead >= jnp.where(i > j - rim_blocks, -BLOCK, 0)
            allowed = later if allowed is None else allowed & later
        dk = dv = None
        for h in range(ratio):
            lanes = slice(h * HEAD_DIM, (h + 1) * HEAD_DIM)
            q_rows, g_rows = q_buf[g, rows, lanes], g_buf[g, rows, lanes]
            scores = dot(k_rows, q_rows, ((1,), (1,)))
            probs = jnp.exp2(scores * (score_scale * LOG2E) - stats[h : h + 1, rows])
            probs = jnp.where(allowed, probs, 0.0)
            grad_prob = dot(v_rows, g_rows, ((1,), (1,)))
            grad_score = (
                probs * (grad_prob - stats[ratio + h : ratio + h + 1, rows])
            ).astype(jnp.bfloat16)
            dv_h = dot(probs.astype(jnp.bfloat16), g_rows, ((1,), (0,)))
            dk_h = dot(grad_score, q_rows, ((1,), (0,)))
            dq_turned[h, :, rows] += dot(k_cols, grad_score, ((1,), (0,)))
            dk = dk_h if dk is None else dk + dk_h
            dv = dv_h if dv is None else dv + dv_h
        sums[g, 0, keys, :] += dk
        sums[g, 1, keys, :] += dv

    def key_block(g, j, in_rim):
        keys = at(j * BLOCK, BLOCK)
        k_turned[:, keys] = k_ext[g, keys, :].astype(jnp.float32).T.astype(jnp.bfloat16)
        sums[g, :, keys, :] = jnp.zeros((2, BLOCK, HEAD_DIM), jnp.float32)
        low, high = jnp.maximum(j - rim_blocks, 0), jnp.minimum(j + 1, q_blocks)
        lax.fori_loop(low, high, lambda i, _: (tile(g, j, i, in_rim), 0)[1], 0)
        if in_rim:
            rim_low[g, :, keys, :] = sums[g, :, keys, :].astype(jnp.bfloat16)

    def prepare(g):
        ones = jnp.ones((8, HEAD_DIM), jnp.bfloat16)
        for h in range(ratio):
            lanes = slice(h * HEAD_DIM, (h + 1) * HEAD_DIM)
            stats[h : h + 1, :] = norm[pl.ds(g * ratio + h, 1), :] * LOG2E

            def rows_of(i, _, h=h, lanes=lanes):
                rows = at(i * BLOCK, BLOCK)
                both = g_buf[g, rows, lanes].astype(jnp.float32) * o_buf[g, rows, lanes].astype(
                    jnp.float32
                )
                high = both.astype(jnp.bfloat16)
                low = (both - high.astype(jnp.float32)).astype(jnp.bfloat16)
                delta = dot(ones, high, ((1,), (1,))) + dot(ones, low, ((1,), (1,)))
                stats[ratio + h : ratio + h + 1, rows] = delta[0:1, :]
                return 0

            lax.fori_loop(0, q_blocks, rows_of, 0)
            dq_turned[h] = jnp.zeros((HEAD_DIM, tokens), jnp.float32)

    def finish_dq(g):
        def rows_of(i, _):
            rows = at(i * BLOCK, BLOCK)
            for h in range(ratio):
                lanes = slice(h * HEAD_DIM, (h + 1) * HEAD_DIM)
                dq_buf[g, rows, lanes] = (dq_turned[h, :, rows].T * score_scale).astype(
                    jnp.bfloat16
                )
            return 0

        lax.fori_loop(0, q_blocks, rows_of, 0)
        for n in range(heads - 1):
            dq_out(g, n).start()
        dq_own(g).start()

    def finish_dkv(g):
        @pl.when(has_after)
        def _():
            rim_out(g).wait_recv()

            def add(i, _):
                rows = at(i * BLOCK, BLOCK)
                own = at(tokens + i * BLOCK, BLOCK)
                for c in range(2):
                    sums[g, c, own, :] += rims[g, c, rows, :].astype(jnp.float32)
                return 0

            lax.fori_loop(0, rim_blocks, add, 0)

        def owner_of(n, _):
            own = at(WINDOW + n * owned, owned)
            dkv_buf[g, n, 0] = (sums[g, 0, own, :] * score_scale).astype(jnp.bfloat16)
            dkv_buf[g, n, 1] = sums[g, 1, own, :].astype(jnp.bfloat16)
            return 0

        lax.fori_loop(0, heads, owner_of, 0)
        for n in range(heads - 1):
            dkv_out(g, n).start()
        dkv_own(g).start()

    barrier = pltpu.get_barrier_semaphore()
    for d in range(1, heads):
        pl.semaphore_signal(
            barrier, inc=1, device_id={"head": lax.rem(z + d, heads)}, device_id_type=MESH
        )

    @pl.when(has_before)
    def _():
        pl.semaphore_signal(barrier, inc=1, device_id={"seq": s - 1}, device_id_type=MESH)

    @pl.when(has_after)
    def _():
        pl.semaphore_signal(barrier, inc=1, device_id={"seq": s + 1}, device_id_type=MESH)

    def start_stage(g, _):
        for n in range(heads - 1):
            stage(g, n).start()
        return 0

    lax.fori_loop(0, groups, start_stage, 0)
    norm_in = pltpu.make_async_copy(n_hbm, norm, norm_sem)
    norm_in.start()
    for copy in inputs(0):
        copy.start()

    pl.semaphore_wait(
        barrier, heads - 1 + has_before.astype(jnp.int32) + has_after.astype(jnp.int32)
    )

    for g in range(min(AHEAD, groups)):
        send_grads(g)
        send_windows(g)
    norm_in.wait()

    def one_group(g, _):
        @pl.when(g + 1 < groups)
        def _():
            for copy in inputs(g + 1):
                copy.start()

        for copy in inputs(g):
            copy.wait()
        for n in range(heads - 1):
            grad_in(g, n, peers[n]).wait_recv()

        @pl.when(g + AHEAD < groups)
        def _():
            send_grads(g + AHEAD)
            send_windows(g + AHEAD)

        prepare(g)

        @pl.when(has_before)
        def _():
            for c in range(2):
                window_in(g, c).wait_recv()
            lax.fori_loop(0, rim_blocks, lambda j, _: (key_block(g, j, True), 0)[1], 0)
            rim_out(g).start()

        @pl.when(g > 0)
        def _():
            finish_dkv(g - 1)

        lax.fori_loop(
            rim_blocks, rim_blocks + q_blocks, lambda j, _: (key_block(g, j, False), 0)[1], 0
        )
        finish_dq(g)
        return 0

    lax.fori_loop(0, groups, one_group, 0)
    finish_dkv(groups - 1)

    def drain(g, _):
        for n in range(heads - 1):
            grad_in(g, n).wait_send()
            dq_out(g, n, peers[n]).wait()
            dkv_out(g, n, peers[n]).wait()
        dq_own(g).wait()
        dkv_own(g).wait()

        @pl.when(has_after)
        def _():
            for c in range(2):
                window_in(g, c).wait_send()

        @pl.when(has_before)
        def _():
            rim_out(g).wait_send()

        return 0

    lax.fori_loop(0, groups, drain, 0)


def write_out(dq_land, dkv_land, dq_hbm, dk_hbm, dv_hbm, sem):
    blocks, _, pair = dq_land.shape

    def copies(n):
        narrow = at(n * HEAD_DIM, HEAD_DIM)
        return [
            pltpu.make_async_copy(dq_land.at[n], dq_hbm.at[:, at(n * pair, pair)], sem.at[n, 0]),
            pltpu.make_async_copy(dkv_land.at[n, 0], dk_hbm.at[:, narrow], sem.at[n, 1]),
            pltpu.make_async_copy(dkv_land.at[n, 1], dv_hbm.at[:, narrow], sem.at[n, 2]),
        ]

    for n in range(blocks):
        for copy in copies(n):
            copy.start()
    for n in range(blocks):
        for copy in copies(n):
            copy.wait()


def on_device(seqs, heads, queries, key_states, value_states, outputs, out_grad, log_norm):
    tokens = queries.shape[0]
    groups = key_states.shape[1] // HEAD_DIM
    ratio = queries.shape[1] // key_states.shape[1]
    pair, owned, span = ratio * HEAD_DIM, tokens // heads, WINDOW + tokens
    low, wide = jnp.bfloat16, jnp.float32
    dma = pltpu.SemaphoreType.DMA
    pairs = groups * ratio * tokens * (WINDOW + BLOCK)
    shapes = [
        (owned, out_grad.shape[1]),
        (owned, key_states.shape[1] * heads),
        (owned, key_states.shape[1] * heads),
    ]
    landed = pl.pallas_call(
        functools.partial(kernel, seqs, heads, groups, ratio, tokens),
        out_shape=[
            pltpu.VMEM((heads * groups, owned, pair), low),
            pltpu.VMEM((heads * groups, 2, owned, HEAD_DIM), low),
        ],
        in_specs=[pl.BlockSpec(memory_space=pltpu.HBM)] * 6,
        out_specs=[pl.BlockSpec(memory_space=pltpu.VMEM)] * 2,
        scratch_shapes=[
            pltpu.VMEM((groups, tokens, pair), low),
            pltpu.VMEM((groups, tokens, pair), low),
            pltpu.VMEM((groups, tokens, pair), low),
            pltpu.VMEM((groups, span, HEAD_DIM), low),
            pltpu.VMEM((groups, span, HEAD_DIM), low),
            pltpu.VMEM(log_norm.shape, wide),
            pltpu.VMEM((2 * ratio, tokens), wide),
            pltpu.VMEM((HEAD_DIM, span), low),
            pltpu.VMEM((ratio, HEAD_DIM, tokens), wide),
            pltpu.VMEM((groups, 2, span, HEAD_DIM), wide),
            pltpu.VMEM((groups, 2, WINDOW, HEAD_DIM), low),
            pltpu.VMEM((groups, 2, WINDOW, HEAD_DIM), low),
            pltpu.VMEM((groups, tokens, pair), low),
            pltpu.VMEM((groups, heads, 2, owned, HEAD_DIM), low),
            pltpu.VMEM((groups, heads - 1, owned, pair), low),
            dma((groups, 5)),
            dma,
            dma((groups, heads)),
            dma((groups, heads)),
            dma((groups, heads)),
            dma((groups, 2)),
            dma((groups, 2)),
            dma((groups,)),
            dma((groups,)),
            dma((groups, heads)),
            dma((groups, heads)),
            dma((groups, heads)),
            dma((groups, heads)),
        ],
        cost_estimate=pl.CostEstimate(
            flops=10 * pairs * HEAD_DIM, bytes_accessed=12 * tokens * 1024, transcendentals=pairs
        ),
        compiler_params=pltpu.CompilerParams(
            collective_id=0, has_side_effects=True, vmem_limit_bytes=52 * 1024 * 1024
        ),
    )(queries, key_states, value_states, outputs, out_grad, log_norm)
    return pl.pallas_call(
        write_out,
        out_shape=[jax.ShapeDtypeStruct(shape, low) for shape in shapes],
        in_specs=[pl.BlockSpec(memory_space=pl.ANY)] * 2,
        out_specs=[pl.BlockSpec(memory_space=pltpu.HBM)] * 3,
        scratch_shapes=[dma((heads * groups, 3))],
        compiler_params=pltpu.CompilerParams(vmem_limit_bytes=1024 * 1024),
    )(*landed)


def solution(mesh):
    placed = (
        P("seq", "head"),
        P("seq", "head"),
        P("seq", "head"),
        P("seq", "head"),
        P(("seq", "head"), None),
        P("head", "seq"),
    )
    return jax.shard_map(
        functools.partial(on_device, mesh.shape["seq"], mesh.shape["head"]),
        mesh=mesh,
        in_specs=placed,
        out_specs=(P(("seq", "head"), None), P(("seq", "head"), None), P(("seq", "head"), None)),
        check_vma=False,
    )
```
